32 devices in a mesh: grp: 2 (over y), rcv: 16 (over z, x, core).
Axes of the slice: x: 2, y: 2, z: 4, core: 2. Of those that a mesh axis runs over, the one named last changes fastest.
Arguments:
- traces: bfloat16 [2, 3072, 5376], P(None, ('grp', 'rcv')), parts along dimension 1, may hold values from -17 to 17, as said below
- sketch: bfloat16 [2, 96, 5376], P(None, None, 'rcv'), may hold values from -0.0625 to 0.0625
Outputs:
- basis: float32 [2, 3072, 96], P(None, ('grp', 'rcv')), parts along dimension 1
- coeffs: float32 [2, 192, 5376], P(None, 'grp', 'rcv'), parts along dimension 1
The draws below stay inside these ranges and needn't reach their ends.
There are 2 independent parts, one for each index of `grp`. The reference program is written for one: setup_inputs(seed, part) draws one part's arguments, and reference() takes and returns one part's arrays. A program takes and returns all parts, laid end to end along the dimension named above; an argument that names none is the same for every part. Nothing has to cross between parts.
Inputs may be any that keep to these rules, and one draw needn't show every extreme that they name: `traces`: complex data, real part at index 0 and imaginary part at index 1 of the first dimension.
All inputs are finite; a program needn't handle non-finite values.
Results may differ from the reference program's by a relative error of at most 0.0015.
Values may be sent and summed in bfloat16 or wider, within the bound.
No kernel may reach another device: no remote copies, remote signals or barrier semaphores. Data moves between devices by JAX's collectives and lax.ppermute only.
A program may use at most 64 MiB of HBM per device.

```python
import math
import jax
import jax.numpy as jnp
from jax import lax

SKETCH = 96
SOURCES = 5376
RECEIVERS = 1536


def draw_traces(key, part):
    first = jax.random.fold_in(key, 11)
    second = jax.random.fold_in(key, 12)
    third = jax.random.fold_in(key, 13)
    places = jnp.arange(RECEIVERS).astype(jnp.float32)
    trend = jnp.exp(-math.log(3.0) * places / max(RECEIVERS - 1, 1))
    base = jnp.clip(jax.random.normal(first, (2, RECEIVERS, SOURCES), jnp.float32), -5.0, 5.0)
    rough = jnp.exp(jax.random.uniform(second, (RECEIVERS,), jnp.float32, 0.0, math.log(3.3)))
    column = jnp.exp(jax.random.uniform(third, (SOURCES,), jnp.float32, math.log(0.5), math.log(2.0)))
    values = base * (trend * rough)[None, :, None] * column[None, None, :] * 0.5
    return values.astype(jnp.bfloat16)


def block_levels(key, extent, split, smallest, largest):
    loudness, own = 1.0, jax.random.fold_in(key, 6)
    for position, shards_of in split:
        heights = jnp.exp(jax.random.uniform(jax.random.fold_in(own, position), (shards_of,), jnp.float32, smallest / len(split), largest / len(split)))
        loudness = loudness * jnp.repeat(heights, extent[position] // shards_of).reshape([-1 if axis == position else 1 for axis in range(len(extent))])
    return loudness


def bell_draw(rng, extent, width, limit, split=(), held_as=jnp.bfloat16):
    drawn = jax.random.normal(rng, extent, jnp.float32) * width
    if len(split) > 0:
        drawn = block_levels(rng, extent, split, -0.22, 0.18) * drawn
    return jnp.clip(drawn, min=-limit, max=limit).astype(held_as)


def setup_inputs(seed: int = 0, part: int = 0) -> dict:
    arg_keys = jax.random.split(jax.random.key(seed), 3)
    own_keys = jax.random.split(jax.random.fold_in(arg_keys[2], part), 3)
    traces = draw_traces(jax.random.fold_in(jax.random.fold_in(arg_keys[2], part), 71), part)
    sketch = bell_draw(arg_keys[1], (2, SKETCH, SOURCES), (2 * SOURCES) ** -0.5, 0.0625, ((2, 16),))
    return dict(traces=traces, sketch=sketch)


def precise_dot(left, right):
    return jnp.dot(left.astype(jnp.float32), right.astype(jnp.float32), precision=lax.Precision.HIGHEST, preferred_element_type=jnp.float32)

def complex_product(left, right):
    return (precise_dot(left[0], right[0]) - precise_dot(left[1], right[1]), precise_dot(left[0], right[1]) + precise_dot(left[1], right[0]))

def adjoint(matrix):
    return (matrix[0].T, -matrix[1].T)

def factor(gram):
    count = gram[0].shape[0]
    embed = jnp.stack([jnp.stack([gram[0], -gram[1]], axis=-1), jnp.stack([gram[1], gram[0]], axis=-1)], axis=1)
    embed = embed.reshape(2 * count, 2 * count)
    lower = jnp.linalg.cholesky(embed)
    ident = jnp.eye(2 * count, dtype=jnp.float32)
    lower_inv = jax.scipy.linalg.solve_triangular(lower, ident, lower=True)
    low_re = lower[0::2, 0::2]
    low_im = lower[1::2, 0::2]
    linv_re = lower_inv[0::2, 0::2]
    linv_im = lower_inv[1::2, 0::2]
    return (low_re.T, -low_im.T, linv_re.T, -linv_im.T)

def reference(traces, sketch):
    data_re = traces[0]
    data_im = traces[1]
    sk_re = sketch[0].T
    sk_im = sketch[1].T
    sk_re_f = jnp.dot(data_re.astype(jnp.float32), sk_re.astype(jnp.float32), preferred_element_type=jnp.float32)
    sketched_re = sk_re_f - jnp.dot(data_im.astype(jnp.float32), sk_im.astype(jnp.float32), preferred_element_type=jnp.float32)
    sketched_im = jnp.dot(data_re.astype(jnp.float32), sk_im.astype(jnp.float32), preferred_element_type=jnp.float32) + jnp.dot(data_im.astype(jnp.float32), sk_re.astype(jnp.float32), preferred_element_type=jnp.float32)
    sketched = (sketched_re, sketched_im)
    gram = complex_product(adjoint(sketched), sketched)
    factors = factor(gram)
    ortho = complex_product(sketched, (factors[2], factors[3]))
    scale = math.sqrt(RECEIVERS)
    basis = jnp.stack([ortho[0] * scale, ortho[1] * scale])
    rounded_re = ortho[0].astype(jnp.bfloat16)
    rounded_im = ortho[1].astype(jnp.bfloat16)
    coef_re = jnp.dot(rounded_re.T.astype(jnp.float32), data_re.astype(jnp.float32), preferred_element_type=jnp.float32) + jnp.dot(rounded_im.T.astype(jnp.float32), data_im.astype(jnp.float32), preferred_element_type=jnp.float32)
    coef_im = jnp.dot(rounded_re.T.astype(jnp.float32), data_im.astype(jnp.float32), preferred_element_type=jnp.float32) - jnp.dot(rounded_im.T.astype(jnp.float32), data_re.astype(jnp.float32), preferred_element_type=jnp.float32)
    return (basis, jnp.stack([coef_re, coef_im]))
```

```python
import functools
import math

import jax
import jax.numpy as jnp
from jax import lax
from jax.experimental import pallas as pl
from jax.experimental.pallas import tpu as pltpu
from jax.sharding import PartitionSpec as P

LANES = 128
ROWS = 8


def axis_masks(size):
    masks = []
    for bit in range(size.bit_length() - 1):
        masks.append(1 << bit if bit < 3 else 3 << (bit - 1))
    return masks


def slot_owner(slot, masks):
    owner = 0
    for bit, mask in enumerate(masks):
        if slot >> bit & 1:
            owner ^= mask
    return owner


def swap(value, mask, size):
    return lax.ppermute(value, "rcv", [(i, i ^ mask) for i in range(size)])


def rotated(items, shift):
    shift = shift % len(items) if items else 0
    return items[shift:] + items[:shift]


def gather_slots(piece, masks, size):
    far = list(range(1, len(masks)))
    ways = max(len(far), 1)
    rows = piece.shape[0]
    cuts = [rows * p // ways // 16 * 16 for p in range(ways)] + [rows]
    parts = [piece[None, cuts[p] : cuts[p + 1]] for p in range(ways)]
    held = [[0] for _ in range(ways)]
    for step in range(len(far)):
        got = []
        for p in range(ways):
            bit = rotated(far, p)[step]
            got.append(swap(parts[p], masks[bit], size))
        for p in range(ways):
            bit = rotated(far, p)[step]
            parts[p] = jnp.concatenate([parts[p], got[p]])
            held[p] = held[p] + [slot | 1 << bit for slot in held[p]]
    if masks:
        for p in range(ways):
            parts[p] = jnp.concatenate([parts[p], swap(parts[p], masks[0], size)])
            held[p] = held[p] + [slot | 1 for slot in held[p]]
    return parts, held


def sketch_kernel(ways, slots, held, owner_ref, data_ref, *refs):
    part_refs, (out_ref, gram_ref) = refs[:ways], refs[ways:]
    count = out_ref.shape[2]
    total = None
    place = [{slot: at for at, slot in enumerate(h)} for h in held]
    for slot in range(slots):
        block = jnp.concatenate([part_refs[p][place[p][slot]] for p in range(ways)], axis=0)
        term = lax.dot_general(
            data_ref[owner_ref[slot]],
            block,
            (((1,), (1,)), ((), ())),
            preferred_element_type=jnp.float32,
        )
        total = term if total is None else total + term
    rows = total.shape[0] // 2
    real = total[:rows, :count] - total[rows:, count:]
    imag = total[:rows, count:] + total[rows:, :count]
    out_ref[0] = real
    out_ref[1] = imag
    exact = functools.partial(
        lax.dot_general,
        dimension_numbers=(((0,), (0,)), ((), ())),
        precision=lax.Precision.HIGHEST,
        preferred_element_type=jnp.float32,
    )
    gram_re = exact(real, real) + exact(imag, imag)
    gram_im = exact(real, imag) - exact(imag, real)
    row = lax.broadcasted_iota(jnp.int32, gram_re.shape, 0)
    column = lax.broadcasted_iota(jnp.int32, gram_re.shape, 1)
    gram_ref[...] = jnp.where(row <= column, gram_re, gram_im)


def eliminate(real, imag):
    count, width = real.shape
    lane = lax.broadcasted_iota(jnp.int32, (ROWS, width), 1)
    row = lax.broadcasted_iota(jnp.int32, (ROWS, width), 0)
    blocks = count // ROWS
    re = [real[ROWS * i : ROWS * (i + 1)] for i in range(blocks)]
    im = [imag[ROWS * i : ROWS * (i + 1)] for i in range(blocks)]
    for b in range(blocks):
        col_re, col_im = [], []
        for o in range(ROWS):
            k = ROWS * b + o
            col_re.append([jnp.broadcast_to(re[i][:, k : k + 1], (ROWS, width)) for i in range(b, blocks)])
            col_im.append([jnp.broadcast_to(im[i][:, k : k + 1], (ROWS, width)) for i in range(b, blocks)])
        for o in range(ROWS):
            hit = lane == ROWS * b + o
            scale = lax.rsqrt(col_re[o][0][o : o + 1])
            pivot_re = jnp.where(hit[:1], scale, re[b][o : o + 1] * scale)
            pivot_im = jnp.where(hit[:1], 0.0, im[b][o : o + 1] * scale)
            by_re = [v * scale for v in col_re[o]]
            by_im = [v * scale for v in col_im[o]]
            for j in range(o + 1, ROWS):
                x_re, x_im = by_re[0][j : j + 1], by_im[0][j : j + 1]
                for q in range(blocks - b):
                    col_re[j][q] = col_re[j][q] - (by_re[q] * x_re + by_im[q] * x_im)
                    col_im[j][q] = col_im[j][q] - (by_im[q] * x_re - by_re[q] * x_im)
            for q, i in enumerate(range(b, blocks)):
                new_re = jnp.where(hit, 0.0, re[i]) - (by_re[q] * pivot_re - by_im[q] * pivot_im)
                new_im = jnp.where(hit, 0.0, im[i]) - (by_re[q] * pivot_im + by_im[q] * pivot_re)
                if i == b:
                    new_re = jnp.where(row > o, new_re, jnp.where(row == o, pivot_re, re[i]))
                    new_im = jnp.where(row > o, new_im, jnp.where(row == o, pivot_im, im[i]))
                re[i], im[i] = new_re, new_im
    return jnp.concatenate(re, axis=0), jnp.concatenate(im, axis=0)


def basis_kernel(scale, gram_ref, sketched_ref, basis_ref, weight_ref):
    packed = gram_ref[...]
    count = packed.shape[0]
    flipped = packed.T
    row = lax.broadcasted_iota(jnp.int32, packed.shape, 0)
    column = lax.broadcasted_iota(jnp.int32, packed.shape, 1)
    gram_re = jnp.where(row <= column, packed, flipped)
    gram_im = jnp.where(row > column, packed, jnp.where(row < column, -flipped, 0.0))
    low_re, low_im = eliminate(gram_re, gram_im)
    low_re = jnp.where(row >= column, low_re, 0.0)
    low_im = jnp.where(row >= column, low_im, 0.0)
    exact = functools.partial(
        lax.dot_general,
        dimension_numbers=(((1,), (1,)), ((), ())),
        precision=lax.Precision.HIGHEST,
        preferred_element_type=jnp.float32,
    )
    real, imag = sketched_ref[0], sketched_ref[1]
    ortho_re = exact(real, low_re) + exact(imag, low_im)
    ortho_im = exact(imag, low_re) - exact(real, low_im)
    basis_ref[0] = ortho_re * scale
    basis_ref[1] = ortho_im * scale
    top = jnp.concatenate([ortho_re.T, ortho_im.T], axis=1)
    low = jnp.concatenate([-ortho_im.T, ortho_re.T], axis=1)
    weight_ref[...] = jnp.concatenate([top, low], axis=0).astype(weight_ref.dtype)


def project_kernel(slots, owner_ref, weight_ref, data_ref, out_ref):
    weight = weight_ref[...]
    for slot in range(slots):
        out_ref[slot] = jnp.dot(
            weight, data_ref[owner_ref[slot]], preferred_element_type=jnp.float32
        )


def scatter_slots(held, masks, size, factor):
    send = lambda value: (value * factor).astype(jnp.float16)
    back = lambda value: value.astype(jnp.float32) / factor
    far = list(range(1, len(masks)))
    ways = max(len(far), 1)
    rows = held.shape[1]
    if masks:
        near = held.reshape((-1, 2) + held.shape[1:])
        held = near[:, 0] + back(swap(send(near[:, 1]), masks[0], size))
    cuts = [rows * p // ways // 16 * 16 for p in range(ways)] + [rows]
    parts = []
    for p in range(ways):
        parts.append(held[:, cuts[p] : cuts[p + 1]].reshape((2,) * len(far) + (cuts[p + 1] - cuts[p], -1)))
    left = [list(reversed(far)) for _ in range(ways)]
    for step in range(len(far)):
        got = []
        for p in range(ways):
            bit = rotated(far, p)[step]
            at = left[p].index(bit)
            got.append(swap(send(lax.index_in_dim(parts[p], 1, at, keepdims=False)), masks[bit], size))
        for p in range(ways):
            bit = rotated(far, p)[step]
            at = left[p].index(bit)
            parts[p] = lax.index_in_dim(parts[p], 0, at, keepdims=False) + back(got[p])
            left[p].remove(bit)
    return jnp.concatenate([part.reshape((-1, part.shape[-1])) for part in parts])


def per_device(traces, sketch):
    size = lax.axis_size("rcv")
    me = lax.axis_index("rcv")
    masks = axis_masks(size)
    rows, sources = traces.shape[1:]
    count, share = sketch.shape[1:]
    vmem = pl.BlockSpec(memory_space=pltpu.VMEM)
    smem = pl.BlockSpec(memory_space=pltpu.SMEM)
    params = pltpu.CompilerParams(vmem_limit_bytes=40 * 1024 * 1024)
    owners = me ^ jnp.array([slot_owner(slot, masks) for slot in range(size)], jnp.int32)

    data = jnp.transpose(traces.reshape(2 * rows, size, share), (1, 0, 2))
    parts, held = gather_slots(sketch.reshape(2 * count, share), masks, size)
    sketched, gram = pl.pallas_call(
        functools.partial(sketch_kernel, len(parts), size, held),
        out_shape=(
            jax.ShapeDtypeStruct((2, rows, count), jnp.float32),
            jax.ShapeDtypeStruct((count, count), jnp.float32),
        ),
        in_specs=[smem] + [vmem] * (1 + len(parts)),
        out_specs=(vmem, vmem),
        compiler_params=params,
        name="sketch_rows",
    )(owners, data, *parts)
    for mask in masks:
        gram = gram + swap(gram, mask, size)
    basis, weight = pl.pallas_call(
        functools.partial(basis_kernel, math.sqrt(rows * size)),
        out_shape=(
            jax.ShapeDtypeStruct((2, rows, count), jnp.float32),
            jax.ShapeDtypeStruct((2 * count, 2 * rows), jnp.bfloat16),
        ),
        in_specs=[vmem, vmem],
        out_specs=(vmem, vmem),
        compiler_params=params,
        name="orthonormal_basis",
    )(gram, sketched)
    terms = pl.pallas_call(
        functools.partial(project_kernel, size),
        out_shape=jax.ShapeDtypeStruct((size, 2 * count, share), jnp.float32),
        in_specs=[smem, vmem, vmem],
        out_specs=vmem,
        compiler_params=params,
        name="project_rows",
    )(owners, weight, data)
    coeffs = scatter_slots(terms, masks, size, jnp.float32(1.0))
    return basis, coeffs.reshape(2, count, share)


def solution(mesh):
    return jax.shard_map(
        per_device,
        mesh=mesh,
        in_specs=(P(None, ("grp", "rcv"), None), P(None, None, "rcv")),
        out_specs=(P(None, ("grp", "rcv"), None), P(None, "grp", "rcv")),
        check_vma=False,
    )
```

```python
import functools
import math

import jax
import jax.numpy as jnp
from jax import lax
from jax.experimental import pallas as pl
from jax.experimental.pallas import tpu as pltpu
from jax.sharding import PartitionSpec as P

ROWS = 8
NEAR = 2
TOP = 32768.0
VMEM = pl.BlockSpec(memory_space=pltpu.VMEM)
SMEM = pl.BlockSpec(memory_space=pltpu.SMEM)
PARAMS = pltpu.CompilerParams(vmem_limit_bytes=40 * 1024 * 1024)


def axis_masks(size):
    masks = []
    for bit in range(size.bit_length() - 1):
        masks.append(1 << bit if bit < 3 else 3 << (bit - 1))
    return masks


def slot_mask(slot, masks):
    away = 0
    for bit, mask in enumerate(masks):
        if slot >> bit & 1:
            away ^= mask
    return away


def swap(value, mask, size):
    return lax.ppermute(value, "rcv", [(i, i ^ mask) for i in range(size)])


def rotated(items, shift):
    return items[shift:] + items[:shift]


def exact(left, right, dims):
    return lax.dot_general(
        left,
        right,
        ((dims[0], dims[1]), ((), ())),
        precision=lax.Precision.HIGHEST,
        preferred_element_type=jnp.float32,
    )


def chunk_kernel(masks, share, me_ref, traces_ref, out_ref, peak_ref):
    rows, sources = traces_ref.shape[1:]
    me = me_ref[0]
    for owner in range(sources // share):
        away = me ^ owner
        slot = 0
        for bit in reversed(range(len(masks))):
            set_ = (away >> bit) & 1
            slot = slot | (set_ << bit)
            away = away ^ (set_ * masks[bit])
        group = slot & ((1 << NEAR) - 1)
        for part in range(2):
            out_ref[group, slot >> NEAR, rows * part : rows * (part + 1), :] = traces_ref[
                part, :, owner * share : (owner + 1) * share
            ]
    peak_ref[...] = jnp.max(jnp.abs(traces_ref[...].astype(jnp.float32)), axis=(0, 1), keepdims=True)[0]


def sketch_kernel(slots, held, data_ref, peak_ref, *refs):
    pieces, (out_ref, gram_ref) = refs[:-2], refs[-2:]
    count = out_ref.shape[2]
    total = None
    for slot in range(slots):
        block = jnp.concatenate([pieces[which][at] for which, at in held[slot]], axis=0)
        term = lax.dot_general(
            data_ref[slot & ((1 << NEAR) - 1), slot >> NEAR],
            block,
            (((1,), (1,)), ((), ())),
            preferred_element_type=jnp.float32,
        )
        total = term if total is None else total + term
    rows = total.shape[0] // 2
    real = total[:rows, :count] - total[rows:, count:]
    imag = total[:rows, count:] + total[rows:, :count]
    out_ref[0] = real
    out_ref[1] = imag
    gram_re = exact(real, real, ((0,), (0,))) + exact(imag, imag, ((0,), (0,)))
    gram_im = exact(real, imag, ((0,), (0,))) - exact(imag, real, ((0,), (0,)))
    row = lax.broadcasted_iota(jnp.int32, gram_re.shape, 0)
    column = lax.broadcasted_iota(jnp.int32, gram_re.shape, 1)
    gram_ref[:, :count] = jnp.where(row <= column, gram_re, gram_im)
    peak = jnp.max(peak_ref[...], axis=1, keepdims=True)
    gram_ref[:, count:] = jnp.broadcast_to(peak, (count, gram_ref.shape[1] - count))


def eliminate(real, imag):
    count, width = real.shape
    lane = lax.broadcasted_iota(jnp.int32, (ROWS, width), 1)
    row = lax.broadcasted_iota(jnp.int32, (ROWS, width), 0)
    blocks = count // ROWS
    re = [real[ROWS * i : ROWS * (i + 1)] for i in range(blocks)]
    im = [imag[ROWS * i : ROWS * (i + 1)] for i in range(blocks)]
    for b in range(blocks):
        col_re, col_im = [], []
        for o in range(ROWS):
            k = ROWS * b + o
            col_re.append([jnp.broadcast_to(re[i][:, k : k + 1], (ROWS, width)) for i in range(b, blocks)])
            col_im.append([jnp.broadcast_to(im[i][:, k : k + 1], (ROWS, width)) for i in range(b, blocks)])
        for o in range(ROWS):
            hit = lane == ROWS * b + o
            scale = lax.rsqrt(col_re[o][0][o : o + 1])
            pivot_re = jnp.where(hit[:1], scale, re[b][o : o + 1] * scale)
            pivot_im = jnp.where(hit[:1], 0.0, im[b][o : o + 1] * scale)
            by_re = [v * scale for v in col_re[o]]
            by_im = [v * scale for v in col_im[o]]
            for j in range(o + 1, ROWS):
                x_re, x_im = by_re[0][j : j + 1], by_im[0][j : j + 1]
                for q in range(blocks - b):
                    col_re[j][q] = col_re[j][q] - (by_re[q] * x_re + by_im[q] * x_im)
                    col_im[j][q] = col_im[j][q] - (by_im[q] * x_re - by_re[q] * x_im)
            for q, i in enumerate(range(b, blocks)):
                new_re = jnp.where(hit, 0.0, re[i]) - (by_re[q] * pivot_re - by_im[q] * pivot_im)
                new_im = jnp.where(hit, 0.0, im[i]) - (by_re[q] * pivot_im + by_im[q] * pivot_re)
                if i == b:
                    new_re = jnp.where(row > o, new_re, jnp.where(row == o, pivot_re, re[i]))
                    new_im = jnp.where(row > o, new_im, jnp.where(row == o, pivot_im, im[i]))
                re[i], im[i] = new_re, new_im
    return jnp.concatenate(re, axis=0), jnp.concatenate(im, axis=0)


def finish_kernel(groups, scale, bound, ways, gram_ref, *refs):
    sketched, data, (basis_ref, *outs) = refs[:groups], refs[groups : 2 * groups], refs[2 * groups :]
    count = gram_ref.shape[0]
    packed = gram_ref[:, :count]
    factor = TOP / (gram_ref[:1, count : count + 1] * bound)
    flipped = packed.T
    row = lax.broadcasted_iota(jnp.int32, packed.shape, 0)
    column = lax.broadcasted_iota(jnp.int32, packed.shape, 1)
    gram_re = jnp.where(row <= column, packed, flipped)
    gram_im = jnp.where(row > column, packed, jnp.where(row < column, -flipped, 0.0))
    low_re, low_im = eliminate(gram_re, gram_im)
    low_re = jnp.where(row >= column, low_re, 0.0)
    low_im = jnp.where(row >= column, low_im, 0.0)
    weights = []
    for group in range(groups):
        real, imag = sketched[group][0], sketched[group][1]
        ortho_re = exact(real, low_re, ((1,), (1,))) + exact(imag, low_im, ((1,), (1,)))
        ortho_im = exact(imag, low_re, ((1,), (1,))) - exact(real, low_im, ((1,), (1,)))
        if group == 0:
            basis_ref[0] = ortho_re * scale
            basis_ref[1] = ortho_im * scale
        flat_re, flat_im = ortho_re.T, ortho_im.T
        top = jnp.concatenate([flat_re, flat_im], axis=1)
        low = jnp.concatenate([-flat_im, flat_re], axis=1)
        weights.append(jnp.concatenate([top, low], axis=0).astype(jnp.bfloat16))
    slots = data[0].shape[0]
    far = list(range(slots.bit_length() - 1))
    rows = 2 * count
    for slot in range(slots):
        total = None
        for group in range(groups):
            term = jnp.dot(weights[group], data[group][slot], preferred_element_type=jnp.float32)
            total = term if total is None else total + term
        for p, (first, last, bit) in enumerate(ways):
            block = total[first:last]
            if bit is None:
                outs[p][0] = block
                continue
            at = (slot >> bit + 1 << bit) | (slot & (1 << bit) - 1)
            if slot >> bit & 1:
                outs[2 * p + 1][at] = block * factor
            else:
                outs[2 * p][at] = block


def per_device(traces, sketch):
    size = lax.axis_size("rcv")
    me = lax.axis_index("rcv")
    masks = axis_masks(size)
    near, far = masks[:NEAR], masks[NEAR:]
    rows, sources = traces.shape[1:]
    count, share = sketch.shape[1:]
    groups, zones = 1 << len(near), 1 << len(far)

    whole = sketch.reshape(1, 2 * count, share)
    whole_slots = [0]
    for bit in range(1, len(near)):
        whole = jnp.concatenate([whole, swap(whole, masks[bit], size)])
        whole_slots = whole_slots + [slot | 1 << bit for slot in whole_slots]

    data, peak = pl.pallas_call(
        functools.partial(chunk_kernel, masks, share),
        out_shape=(
            jax.ShapeDtypeStruct((groups, zones, 2 * rows, share), traces.dtype),
            jax.ShapeDtypeStruct((1, sources), jnp.float32),
        ),
        in_specs=[SMEM, VMEM],
        out_specs=(VMEM, VMEM),
        compiler_params=PARAMS,
        name="source_chunks",
    )(me.reshape(1), traces)
    traded = [data[0]] + [swap(data[g], slot_mask(g, masks), size) for g in range(1, groups)]

    ways = max(len(far), 1)
    cuts = [2 * count * p // ways // 16 * 16 for p in range(ways)] + [2 * count]
    pieces, held = [], [[None] * ways for _ in range(size)]
    parts = [whole[:, cuts[p] : cuts[p + 1]] for p in range(ways)]
    owns = [list(whole_slots) for _ in range(ways)]
    order = [rotated(list(range(NEAR, len(masks))), p) if far else [] for p in range(ways)]

    def settle(p, piece, slots):
        for which, extra in ((piece, 0), (swap(piece, masks[0], size), 1)) if masks else ((piece, 0),):
            for at, slot in enumerate(slots):
                held[slot | extra][p] = (len(pieces), at)
            pieces.append(which)

    for step in range(len(far)):
        got = [swap(parts[p], masks[order[p][step]], size) for p in range(ways)]
        for p in range(ways):
            bit = order[p][step]
            fresh = [slot | 1 << bit for slot in owns[p]]
            if step == len(far) - 1:
                settle(p, parts[p], owns[p])
                settle(p, got[p], fresh)
            else:
                parts[p] = jnp.concatenate([parts[p], got[p]])
            owns[p] = owns[p] + fresh
    if not far:
        settle(0, parts[0], owns[0])

    sketched, gram = pl.pallas_call(
        functools.partial(sketch_kernel, size, held),
        out_shape=(
            jax.ShapeDtypeStruct((2, rows, count), jnp.float32),
            jax.ShapeDtypeStruct((count, count + 1), jnp.float32),
        ),
        in_specs=[VMEM] * (2 + len(pieces)),
        out_specs=(VMEM, VMEM),
        compiler_params=PARAMS,
        name="sketch_rows",
    )(data, peak, *pieces)
    known = [sketched] + [swap(sketched, slot_mask(g, masks), size) for g in range(1, groups)]
    for mask in masks[:1] + masks[:0:-1]:
        gram = gram + swap(gram, mask, size)

    bound = 1.01 * math.sqrt(2 * rows * size)
    plan = [(cuts[p], cuts[p + 1], order[p][0] - NEAR if far else None) for p in range(ways)]
    shapes = []
    for first, last, bit in plan:
        shape = (max(zones // 2, 1), last - first, share)
        shapes.append(jax.ShapeDtypeStruct(shape, jnp.float32))
        if bit is not None:
            shapes.append(jax.ShapeDtypeStruct(shape, jnp.float32))
    basis, *sums = pl.pallas_call(
        functools.partial(finish_kernel, groups, math.sqrt(rows * size), bound, plan),
        out_shape=(jax.ShapeDtypeStruct((2, rows, count), jnp.float32), *shapes),
        in_specs=[VMEM] * (1 + 2 * groups),
        out_specs=(VMEM,) * (1 + len(shapes)),
        compiler_params=PARAMS,
        name="basis_and_projection",
    )(gram, *known, *traded)

    if far:
        level = gram[0, count] * bound
        factor, back = TOP / level, level / TOP
        keep, send = list(sums[0::2]), [v.astype(jnp.float16) for v in sums[1::2]]
        left = [sorted(order[p][1:], reverse=True) for p in range(ways)]
        for step in range(len(far)):
            got = [swap(send[p], masks[order[p][step]], size) for p in range(ways)]
            for p in range(ways):
                total = keep[p] + got[p].astype(jnp.float32) * back
                if step < len(far) - 1:
                    bit = order[p][step + 1]
                    at = left[p].index(bit)
                    shape = total.shape
                    halves = total.reshape((2 ** at, 2, -1) + shape[1:])
                    keep[p] = halves[:, 0].reshape((-1,) + shape[1:])
                    send[p] = (halves[:, 1].reshape((-1,) + shape[1:]) * factor).astype(jnp.float16)
                    left[p].remove(bit)
                else:
                    keep[p] = total
        sums = keep
    coeffs = jnp.concatenate([part[0] for part in sums]) if len(sums) > 1 else sums[0][0]
    return basis, coeffs.reshape(2, count, share)


def solution(mesh):
    return jax.shard_map(
        per_device,
        mesh=mesh,
        in_specs=(P(None, ("grp", "rcv"), None), P(None, None, "rcv")),
        out_specs=(P(None, ("grp", "rcv"), None), P(None, "grp", "rcv")),
        check_vma=False,
    )
```

```python
import functools
import math

import jax
import jax.numpy as jnp
from jax import lax
from jax.experimental import pallas as pl
from jax.experimental.pallas import tpu as pltpu
from jax.sharding import PartitionSpec as P

ROWS = 8
NEAR = 2
TOP = 32768.0
VMEM = pl.BlockSpec(memory_space=pltpu.VMEM)
SMEM = pl.BlockSpec(memory_space=pltpu.SMEM)
PARAMS = pltpu.CompilerParams(vmem_limit_bytes=40 * 1024 * 1024)


def swap(value, mask, size):
    return lax.ppermute(value, "rcv", [(i, i ^ mask) for i in range(size)])


def exact(left, right, dims):
    return lax.dot_general(
        left,
        right,
        ((dims[0], dims[1]), ((), ())),
        precision=lax.Precision.HIGHEST,
        preferred_element_type=jnp.float32,
    )


def chunk_kernel(share, me_ref, traces_ref, *refs):
    groups, peak_ref = refs[:-1], refs[-1]
    rows, sources = traces_ref.shape[1:]
    me = me_ref[0]
    near = len(groups)
    for block in range(sources // share // near):
        for member in range(near):
            owner = block * near + member
            away = member ^ (me & (near - 1))
            slot = block ^ (me // near)
            for group in range(near):

                @pl.when(away == group)
                def _(group=group, owner=owner, slot=slot):
                    for part in range(2):
                        groups[group][slot, rows * part : rows * (part + 1), :] = traces_ref[
                            part, :, owner * share : (owner + 1) * share
                        ]

    peak_ref[...] = jnp.max(jnp.abs(traces_ref[...].astype(jnp.float32)), axis=(0, 1), keepdims=True)[0]


def sketch_kernel(slots, groups, held, *refs):
    data, peak_ref, pieces, (out_ref, gram_ref) = refs[:groups], refs[groups], refs[groups + 1 : -2], refs[-2:]
    count = out_ref.shape[2]
    total = None
    for slot in range(slots):
        which, at = held[slot]
        term = lax.dot_general(
            data[slot % groups][slot // groups],
            pieces[which][at],
            (((1,), (1,)), ((), ())),
            preferred_element_type=jnp.float32,
        )
        total = term if total is None else total + term
    rows = total.shape[0] // 2
    real = total[:rows, :count] - total[rows:, count:]
    imag = total[:rows, count:] + total[rows:, :count]
    out_ref[0] = real
    out_ref[1] = imag
    gram_re = exact(real, real, ((0,), (0,))) + exact(imag, imag, ((0,), (0,)))
    gram_im = exact(real, imag, ((0,), (0,))) - exact(imag, real, ((0,), (0,)))
    row = lax.broadcasted_iota(jnp.int32, gram_re.shape, 0)
    column = lax.broadcasted_iota(jnp.int32, gram_re.shape, 1)
    gram_ref[:, :count] = jnp.where(row <= column, gram_re, gram_im)
    peak = jnp.max(peak_ref[...], axis=1, keepdims=True)
    gram_ref[:, count:] = jnp.broadcast_to(peak, (count, gram_ref.shape[1] - count))


def eliminate(real, imag):
    count, width = real.shape
    lane = lax.broadcasted_iota(jnp.int32, (ROWS, width), 1)
    row = lax.broadcasted_iota(jnp.int32, (ROWS, width), 0)
    blocks = count // ROWS
    re = [real[ROWS * i : ROWS * (i + 1)] for i in range(blocks)]
    im = [imag[ROWS * i : ROWS * (i + 1)] for i in range(blocks)]
    for b in range(blocks):
        col_re, col_im = [], []
        for o in range(ROWS):
            k = ROWS * b + o
            col_re.append([jnp.broadcast_to(re[i][:, k : k + 1], (ROWS, width)) for i in range(b, blocks)])
            col_im.append([jnp.broadcast_to(im[i][:, k : k + 1], (ROWS, width)) for i in range(b, blocks)])
        for o in range(ROWS):
            hit = lane == ROWS * b + o
            scale = lax.rsqrt(col_re[o][0][o : o + 1])
            pivot_re = jnp.where(hit[:1], scale, re[b][o : o + 1] * scale)
            pivot_im = jnp.where(hit[:1], 0.0, im[b][o : o + 1] * scale)
            by_re = [v * scale for v in col_re[o]]
            by_im = [v * scale for v in col_im[o]]
            for j in range(o + 1, ROWS):
                x_re, x_im = by_re[0][j : j + 1], by_im[0][j : j + 1]
                for q in range(blocks - b):
                    col_re[j][q] = col_re[j][q] - (by_re[q] * x_re + by_im[q] * x_im)
                    col_im[j][q] = col_im[j][q] - (by_im[q] * x_re - by_re[q] * x_im)
            for q, i in enumerate(range(b, blocks)):
                new_re = jnp.where(hit, 0.0, re[i]) - (by_re[q] * pivot_re - by_im[q] * pivot_im)
                new_im = jnp.where(hit, 0.0, im[i]) - (by_re[q] * pivot_im + by_im[q] * pivot_re)
                if i == b:
                    new_re = jnp.where(row > o, new_re, jnp.where(row == o, pivot_re, re[i]))
                    new_im = jnp.where(row > o, new_im, jnp.where(row == o, pivot_im, im[i]))
                re[i], im[i] = new_re, new_im
    return jnp.concatenate(re, axis=0), jnp.concatenate(im, axis=0)


def finish_kernel(groups, scale, bound, gram_ref, *refs):
    sketched, data, (basis_ref, *outs) = refs[:groups], refs[groups : 2 * groups], refs[2 * groups :]
    count = gram_ref.shape[0]
    packed = gram_ref[:, :count]
    factor = TOP / (gram_ref[:1, count : count + 1] * bound)
    flipped = packed.T
    row = lax.broadcasted_iota(jnp.int32, packed.shape, 0)
    column = lax.broadcasted_iota(jnp.int32, packed.shape, 1)
    gram_re = jnp.where(row <= column, packed, flipped)
    gram_im = jnp.where(row > column, packed, jnp.where(row < column, -flipped, 0.0))
    low_re, low_im = eliminate(gram_re, gram_im)
    low_re = jnp.where(row >= column, low_re, 0.0)
    low_im = jnp.where(row >= column, low_im, 0.0)
    stacked = jnp.concatenate([ref[part] for ref in sketched for part in range(2)], axis=0)
    by_re = exact(stacked, low_re, ((1,), (1,)))
    by_im = exact(stacked, low_im, ((1,), (1,)))
    rows = stacked.shape[0] // groups // 2
    weights = []
    for group in range(groups):
        real = slice(2 * rows * group, 2 * rows * group + rows)
        imag = slice(2 * rows * group + rows, 2 * rows * (group + 1))
        ortho_re = by_re[real] + by_im[imag]
        ortho_im = by_re[imag] - by_im[real]
        if group == 0:
            basis_ref[0] = ortho_re * scale
            basis_ref[1] = ortho_im * scale
        flat_re, flat_im = ortho_re.T, ortho_im.T
        top = jnp.concatenate([flat_re, flat_im], axis=1)
        low = jnp.concatenate([-flat_im, flat_re], axis=1)
        weights.append(jnp.concatenate([top, low], axis=0).astype(jnp.bfloat16))
    for slot in range(data[0].shape[0]):
        total = None
        for group in range(groups):
            term = jnp.dot(weights[group], data[group][slot], preferred_element_type=jnp.float32)
            total = term if total is None else total + term
        outs[slot][...] = total if slot == 0 else total * factor


def tied(first, second):
    first, second = list(first), list(second)
    both = lax.optimization_barrier(tuple(first + second))
    return list(both[: len(first)]), list(both[len(first) :])


def gather_slots(piece, size):
    bits = size.bit_length() - 1
    direct = range(1, min(bits, 4))
    have = {0: piece}
    for level in range(1, len(direct) + 1):
        for slot in range(0, 1 << (direct.stop if bits > 1 else 1), 2):
            if slot.bit_count() == level:
                low = slot & -slot
                have[slot] = swap(have[slot ^ low], low, size)
    pieces = [(have[slot], [slot]) for slot in sorted(have, key=lambda slot: (slot.bit_count(), slot))]
    for bit in range(4, bits):
        whole = jnp.concatenate([value for value, _ in pieces])
        slots = [slot for _, held in pieces for slot in held]
        pieces = [(whole, slots), (swap(whole, 1 << bit, size), [slot | 1 << bit for slot in slots])]
    if bits:
        pieces += [(swap(value, 1, size), [slot | 1 for slot in slots]) for value, slots in pieces]
    return pieces


def sum_all(value, size, tie):
    bits = size.bit_length() - 1
    steps = [[1]] if bits else []
    if bits > 2:
        steps.append([2, 4])
    steps += [[1 << bit] for bit in range(3 if bits > 2 else 1, bits)]
    for at, step in enumerate(steps):
        if at == len(steps) - 1:
            value = tie(value)
        if len(step) == 2:
            first, second = step
            near = value + swap(value, first, size)
            value = near + (swap(value, second, size) + swap(value, first | second, size))
        else:
            value = value + swap(value, step[0], size)
    return value


def per_device(traces, sketch):
    size = lax.axis_size("rcv")
    me = lax.axis_index("rcv")
    rows, sources = traces.shape[1:]
    count, share = sketch.shape[1:]
    groups = min(1 << NEAR, size)
    zones = size // groups

    pieces = gather_slots(sketch.reshape(1, 2 * count, share), size)
    *data, peak = pl.pallas_call(
        functools.partial(chunk_kernel, share),
        out_shape=(jax.ShapeDtypeStruct((zones, 2 * rows, share), traces.dtype),) * groups
        + (jax.ShapeDtypeStruct((1, sources), jnp.float32),),
        in_specs=[SMEM, VMEM],
        out_specs=(VMEM,) * (groups + 1),
        compiler_params=PARAMS,
        name="source_chunks",
    )(me.astype(jnp.int32).reshape(1), traces)
    traded = [swap(data[group], group, size) for group in range(1, groups)]

    values, traded[:2] = tied([value for value, _ in pieces], traded[:2])
    held = {slot: (which, at) for which, (_, slots) in enumerate(pieces) for at, slot in enumerate(slots)}
    sketched, gram = pl.pallas_call(
        functools.partial(sketch_kernel, size, groups, held),
        out_shape=(
            jax.ShapeDtypeStruct((2, rows, count), jnp.float32),
            jax.ShapeDtypeStruct((count, count + 1), jnp.float32),
        ),
        in_specs=[VMEM] * (groups + 1 + len(values)),
        out_specs=(VMEM, VMEM),
        compiler_params=PARAMS,
        name="sketch_rows",
    )(*data, peak, *values)
    known = [swap(sketched, group, size) for group in range(1, groups)]

    def tie(value):
        nonlocal known, traded
        (value,), rest = tied([value], known + traded)
        known, traded = rest[: len(known)], rest[len(known) :]
        return value

    gram = sum_all(gram, size, tie)

    bound = 1.01 * math.sqrt(2 * rows * size)
    basis, *terms = pl.pallas_call(
        functools.partial(finish_kernel, groups, math.sqrt(rows * size), bound),
        out_shape=(jax.ShapeDtypeStruct((2, rows, count), jnp.float32),)
        + (jax.ShapeDtypeStruct((2 * count, share), jnp.float32),) * zones,
        in_specs=[VMEM] * (1 + 2 * groups),
        out_specs=(VMEM,) * (1 + zones),
        compiler_params=PARAMS,
        name="basis_and_projection",
    )(gram, sketched, *known, data[0], *traded)

    level = gram[0, count] * bound
    total = terms[0]
    if zones <= 4:
        parts = [swap(terms[zone].astype(jnp.float16), zone * groups, size) for zone in range(1, zones)]
    else:
        held_terms = jnp.stack([total * (TOP / level)] + terms[1:])
        parts = []
        for bit in reversed(range(zones.bit_length() - 1)):
            low, high = jnp.split(held_terms, 2)
            got = swap(high.astype(jnp.float16), groups << bit, size)
            held_terms = low + got.astype(jnp.float32)
        total = held_terms[0] * (level / TOP)
    if parts:
        total = total + sum(part.astype(jnp.float32) for part in parts) * (level / TOP)
    return basis, total.reshape(2, count, share)


def solution(mesh):
    return jax.shard_map(
        per_device,
        mesh=mesh,
        in_specs=(P(None, ("grp", "rcv"), None), P(None, None, "rcv")),
        out_specs=(P(None, ("grp", "rcv"), None), P(None, "grp", "rcv")),
        check_vma=False,
    )
```

```python
import functools
import math

import jax
import jax.numpy as jnp
from jax import lax
from jax.experimental import pallas as pl
from jax.experimental.pallas import tpu as pltpu
from jax.sharding import PartitionSpec as P

ROWS = 8
GROUPS = 4
TOP = 32768.0
VMEM = pl.BlockSpec(memory_space=pltpu.VMEM)
SMEM = pl.BlockSpec(memory_space=pltpu.SMEM)
PARAMS = pltpu.CompilerParams(vmem_limit_bytes=40 * 1024 * 1024)


def swap(value, mask, size):
    return lax.ppermute(value, "rcv", [(i, i ^ mask) for i in range(size)])


def exact(left, right, dims):
    return lax.dot_general(
        left,
        right,
        ((dims[0], dims[1]), ((), ())),
        precision=lax.Precision.HIGHEST,
        preferred_element_type=jnp.float32,
    )


def chunk_kernel(share, me_ref, traces_ref, stay_ref, core_ref, near_ref, far_ref, cross_ref, peak_ref, held_ref):
    rows, sources = traces_ref.shape[1:]
    me = me_ref[0]
    for owner in range(sources // share):
        away = owner ^ me
        for part in range(2):
            held_ref[away % GROUPS, away // GROUPS, rows * part : rows * (part + 1), :] = traces_ref[
                part, :, owner * share : (owner + 1) * share
            ]
    zones = stay_ref.shape[0]
    half = zones // 2
    stay_ref[...] = held_ref[0]
    core_ref[:zones] = held_ref[1]
    core_ref[zones:] = held_ref[3, :half]
    near_ref[...] = held_ref[2, :half]
    far_ref[...] = held_ref[2, half:]
    cross_ref[...] = held_ref[3, half:]
    peak = jnp.maximum(
        jnp.max(jnp.abs(traces_ref[0]), axis=0, keepdims=True),
        jnp.max(jnp.abs(traces_ref[1]), axis=0, keepdims=True),
    )
    peak_ref[...] = peak.astype(jnp.float32)


def sketch_kernel(held, stay_ref, core_ref, near_ref, far_ref, cross_ref, peak_ref, *refs):
    pieces, (out_ref, gram_ref) = refs[:-2], refs[-2:]
    count = out_ref.shape[2]
    zones = stay_ref.shape[0]
    half = zones // 2
    total = None
    for slot in range(GROUPS * zones):
        group, zone = slot % GROUPS, slot // GROUPS
        if group < 2:
            data = (stay_ref, core_ref)[group][zone]
        elif zone < half:
            data = near_ref[zone] if group == 2 else core_ref[zones + zone]
        else:
            data = (far_ref, cross_ref)[group - 2][zone - half]
        which, at = held[slot]
        term = lax.dot_general(
            data, pieces[which][at], (((1,), (1,)), ((), ())), preferred_element_type=jnp.float32
        )
        total = term if total is None else total + term
    rows = total.shape[0] // 2
    real = total[:rows, :count] - total[rows:, count:]
    imag = total[:rows, count:] + total[rows:, :count]
    out_ref[0] = real
    out_ref[1] = imag
    gram_re = exact(real, real, ((0,), (0,))) + exact(imag, imag, ((0,), (0,)))
    gram_im = exact(real, imag, ((0,), (0,))) - exact(imag, real, ((0,), (0,)))
    row = lax.broadcasted_iota(jnp.int32, gram_re.shape, 0)
    column = lax.broadcasted_iota(jnp.int32, gram_re.shape, 1)
    gram_ref[:, :count] = jnp.where(row <= column, gram_re, gram_im)
    peak = jnp.max(peak_ref[...], axis=1, keepdims=True)
    gram_ref[:, count:] = jnp.broadcast_to(peak, (count, gram_ref.shape[1] - count))


def eliminate(real, imag):
    count, width = real.shape
    lane = lax.broadcasted_iota(jnp.int32, (ROWS, width), 1)
    row = lax.broadcasted_iota(jnp.int32, (ROWS, width), 0)
    blocks = count // ROWS
    re = [real[ROWS * i : ROWS * (i + 1)] for i in range(blocks)]
    im = [imag[ROWS * i : ROWS * (i + 1)] for i in range(blocks)]
    for b in range(blocks):
        col_re, col_im = [], []
        for o in range(ROWS):
            k = ROWS * b + o
            col_re.append([jnp.broadcast_to(re[i][:, k : k + 1], (ROWS, width)) for i in range(b, blocks)])
            col_im.append([jnp.broadcast_to(im[i][:, k : k + 1], (ROWS, width)) for i in range(b, blocks)])
        for o in range(ROWS):
            hit = lane == ROWS * b + o
            scale = lax.rsqrt(col_re[o][0][o : o + 1])
            pivot_re = jnp.where(hit[:1], scale, re[b][o : o + 1] * scale)
            pivot_im = jnp.where(hit[:1], 0.0, im[b][o : o + 1] * scale)
            by_re = [v * scale for v in col_re[o]]
            by_im = [v * scale for v in col_im[o]]
            for j in range(o + 1, ROWS):
                x_re, x_im = by_re[0][j : j + 1], by_im[0][j : j + 1]
                for q in range(blocks - b):
                    col_re[j][q] = col_re[j][q] - (by_re[q] * x_re + by_im[q] * x_im)
                    col_im[j][q] = col_im[j][q] - (by_im[q] * x_re - by_re[q] * x_im)
            for q, i in enumerate(range(b, blocks)):
                new_re = jnp.where(hit, 0.0, re[i]) - (by_re[q] * pivot_re - by_im[q] * pivot_im)
                new_im = jnp.where(hit, 0.0, im[i]) - (by_re[q] * pivot_im + by_im[q] * pivot_re)
                if i == b:
                    new_re = jnp.where(row > o, new_re, jnp.where(row == o, pivot_re, re[i]))
                    new_im = jnp.where(row > o, new_im, jnp.where(row == o, pivot_im, im[i]))
                re[i], im[i] = new_re, new_im
    return jnp.concatenate(re, axis=0), jnp.concatenate(im, axis=0)


def basis_kernel(scale, gram_ref, *refs):
    sketched, basis_ref, weights = refs[:GROUPS], refs[GROUPS], refs[GROUPS + 1 :]
    count = gram_ref.shape[0]
    packed = gram_ref[:, :count]
    flipped = packed.T
    row = lax.broadcasted_iota(jnp.int32, packed.shape, 0)
    column = lax.broadcasted_iota(jnp.int32, packed.shape, 1)
    gram_re = jnp.where(row <= column, packed, flipped)
    gram_im = jnp.where(row > column, packed, jnp.where(row < column, -flipped, 0.0))
    low_re, low_im = eliminate(gram_re, gram_im)
    low_re = jnp.where(row >= column, low_re, 0.0)
    low_im = jnp.where(row >= column, low_im, 0.0)
    stacked = jnp.concatenate([ref[part] for ref in sketched for part in range(2)], axis=0)
    by_re = exact(stacked, low_re, ((1,), (1,)))
    by_im = exact(stacked, low_im, ((1,), (1,)))
    rows = stacked.shape[0] // GROUPS // 2
    for group in range(GROUPS):
        real = slice(2 * rows * group, 2 * rows * group + rows)
        imag = slice(2 * rows * group + rows, 2 * rows * (group + 1))
        ortho_re = by_re[real] + by_im[imag]
        ortho_im = by_re[imag] - by_im[real]
        if group == 0:
            basis_ref[0] = ortho_re * scale
            basis_ref[1] = ortho_im * scale
        flat_re, flat_im = ortho_re.T, ortho_im.T
        top = jnp.concatenate([flat_re, flat_im], axis=1)
        low = jnp.concatenate([-flat_im, flat_re], axis=1)
        weights[group][...] = jnp.concatenate([top, low], axis=0).astype(jnp.bfloat16)


def project_kernel(bound, gram_ref, *refs):
    weights, (stay_ref, core_ref, near_ref, far_ref, cross_ref) = refs[:GROUPS], refs[GROUPS : GROUPS + 5]
    own_ref, side_ref, *far_outs = refs[GROUPS + 5 :]
    count = gram_ref.shape[0]
    factor = TOP / (gram_ref[:1, count : count + 1] * bound)
    half = near_ref.shape[0]
    zones = 2 * half

    def project(*data):
        total = None
        for weight_ref, block in zip(weights, data):
            term = jnp.dot(weight_ref[...], block, preferred_element_type=jnp.float32)
            total = term if total is None else total + term
        return total * factor

    for zone in range(half):
        far_outs[zone][...] = project(stay_ref[half + zone], core_ref[half + zone], far_ref[zone], cross_ref[zone])
    for zone in range(half):
        side_ref[zone] = project(near_ref[zone], core_ref[zones + zone])
        own_ref[zone] = project(stay_ref[zone], core_ref[zone])


def tied(first, second):
    first, second = list(first), list(second)
    both = lax.optimization_barrier(tuple(first + second))
    return list(both[: len(first)]), list(both[len(first) :])


def gather_slots(piece, size, ahead):
    bits = size.bit_length() - 1
    direct = min(bits, 4)
    have = {0: piece}
    for level in range(1, direct):
        if level == 2:
            (have[1 << direct - 1],), _ = tied([have[1 << direct - 1]], [ahead])
        for slot in reversed(range(0, 1 << direct, 2)):
            if slot.bit_count() == level:
                along = slot & -slot if slot >> direct - 1 else 1 << slot.bit_length() - 1
                have[slot] = swap(have[slot ^ along], along, size)
    pieces = [(have[slot], [slot]) for slot in sorted(have, key=lambda slot: (slot.bit_count(), slot))]
    for bit in range(4, bits):
        whole = jnp.concatenate([value for value, _ in pieces])
        slots = [slot for _, held in pieces for slot in held]
        pieces = [(whole, slots), (swap(whole, 1 << bit, size), [slot | 1 << bit for slot in slots])]
    return pieces + [(swap(value, 1, size), [slot | 1 for slot in slots]) for value, slots in pieces]


def per_device(traces, sketch):
    size = lax.axis_size("rcv")
    me = lax.axis_index("rcv")
    rows, sources = traces.shape[1:]
    count, share = sketch.shape[1:]
    zones = size // GROUPS
    half = zones // 2
    bits = size.bit_length() - 1
    chunk = lambda slots: jax.ShapeDtypeStruct((slots, 2 * rows, share), traces.dtype)

    stay, core, near, far, cross, peak = pl.pallas_call(
        functools.partial(chunk_kernel, share),
        out_shape=(
            chunk(zones),
            chunk(zones + half),
            chunk(half),
            chunk(half),
            chunk(half),
            jax.ShapeDtypeStruct((1, sources), jnp.float32),
        ),
        in_specs=[SMEM, VMEM],
        out_specs=(VMEM,) * 6,
        scratch_shapes=[pltpu.VMEM((GROUPS, zones, 2 * rows, share), traces.dtype)],
        compiler_params=PARAMS,
        name="source_chunks",
    )(me.astype(jnp.int32).reshape(1), traces)
    pieces = gather_slots(sketch.reshape(1, 2 * count, share), size, stay)
    values = [value for value, _ in pieces]
    held = {slot: (which, at) for which, (_, slots) in enumerate(pieces) for at, slot in enumerate(slots)}
    sketched, gram = pl.pallas_call(
        functools.partial(sketch_kernel, held),
        out_shape=(
            jax.ShapeDtypeStruct((2, rows, count), jnp.float32),
            jax.ShapeDtypeStruct((count, count + 1), jnp.float32),
        ),
        in_specs=[VMEM] * (6 + len(values)),
        out_specs=(VMEM, VMEM),
        compiler_params=PARAMS,
        name="sketch_rows",
    )(stay, core, near, far, cross, peak, *values)

    core_in = swap(core, 1, size)
    gram = gram + swap(gram, 1, size)
    beside = swap(gram, 2, size)
    known = [swap(sketched, group, size) for group in range(1, GROUPS)]
    (far_out, cross_out), _ = tied([far, cross], [beside, *known])
    far_in, cross_in = swap(far_out, 2, size), swap(cross_out, 3, size)
    gram = gram + beside
    for bit in range(2, bits):
        gram = gram + swap(gram, 1 << bit, size)

    basis, *weights = pl.pallas_call(
        functools.partial(basis_kernel, math.sqrt(rows * size)),
        out_shape=(jax.ShapeDtypeStruct((2, rows, count), jnp.float32),)
        + (jax.ShapeDtypeStruct((2 * count, 2 * rows), jnp.bfloat16),) * GROUPS,
        in_specs=[VMEM] * (1 + GROUPS),
        out_specs=(VMEM,) * (1 + GROUPS),
        compiler_params=PARAMS,
        name="orthonormal_basis",
    )(gram, sketched, *known)
    bound = 1.01 * math.sqrt(2 * rows * size)
    own, side, *away = pl.pallas_call(
        functools.partial(project_kernel, bound),
        out_shape=(
            jax.ShapeDtypeStruct((half, 2 * count, share), jnp.float32),
            jax.ShapeDtypeStruct((half, 2 * count, share), jnp.float32),
        )
        + (jax.ShapeDtypeStruct((2 * count, share), jnp.float32),) * half,
        in_specs=[VMEM] * (1 + GROUPS + 5),
        out_specs=(VMEM,) * (2 + half),
        compiler_params=PARAMS,
        name="project_rows",
    )(gram, *weights, stay, core_in, near, far_in, cross_in)

    send = lambda value, mask: swap(value.astype(jnp.float16), mask, size).astype(jnp.float32)
    if zones <= 4:
        total = sum(send(value, GROUPS * (half + zone)) for zone, value in enumerate(away))
        side = send(side, 2)
        for zone in range(1, half):
            total = total + send(own[zone] + side[zone], GROUPS * zone)
        total = total + (own[0] + side[0])
    else:
        total = own + send(side, 2) + send(jnp.stack(away), GROUPS * half)
        while total.shape[0] > 1:
            low, high = jnp.split(total, 2)
            total = low + send(high, GROUPS * low.shape[0])
        total = total[0]
    level = gram[0, count] * bound
    return basis, (total * (level / TOP)).reshape(2, count, share)


def solution(mesh):
    return jax.shard_map(
        per_device,
        mesh=mesh,
        in_specs=(P(None, ("grp", "rcv"), None), P(None, None, "rcv")),
        out_specs=(P(None, ("grp", "rcv"), None), P(None, "grp", "rcv")),
        check_vma=False,
    )
```

```python
import functools
import math

import jax
import jax.numpy as jnp
from jax import lax
from jax.experimental import pallas as pl
from jax.experimental.pallas import tpu as pltpu
from jax.sharding import PartitionSpec as P

ROWS = 8
GROUPS = 4
PARTS = 4
TOP = 32768.0
VMEM = pl.BlockSpec(memory_space=pltpu.VMEM)
SMEM = pl.BlockSpec(memory_space=pltpu.SMEM)
PARAMS = pltpu.CompilerParams(vmem_limit_bytes=40 * 1024 * 1024)


def swap(value, mask, size):
    return lax.ppermute(value, "rcv", [(i, i ^ mask) for i in range(size)])


def exact(left, right, dims):
    return lax.dot_general(
        left,
        right,
        ((dims[0], dims[1]), ((), ())),
        precision=lax.Precision.HIGHEST,
        preferred_element_type=jnp.float32,
    )


def chunk_kernel(share, me_ref, traces_ref, stay_ref, near_ref, far_ref, cross_ref, peak_ref, *refs):
    core, held_ref = refs[:-1], refs[-1]
    rows, sources = traces_ref.shape[1:]
    me = me_ref[0]
    for owner in range(sources // share):
        away = owner ^ me
        for part in range(2):
            held_ref[away % GROUPS, away // GROUPS, rows * part : rows * (part + 1), :] = traces_ref[
                part, :, owner * share : (owner + 1) * share
            ]
    zones, half = stay_ref.shape[0], near_ref.shape[0]
    for at, ref in enumerate(core):
        first = at % PARTS * ref.shape[0]
        ref[...] = held_ref[1 + at // PARTS * 2, first : first + ref.shape[0]]
    stay_ref[...] = held_ref[0]
    near_ref[...] = held_ref[2, :half]
    far_ref[...] = held_ref[2, half:]
    cross_ref[...] = held_ref[3, half:]
    peak = jnp.maximum(
        jnp.max(jnp.abs(traces_ref[0]), axis=0, keepdims=True),
        jnp.max(jnp.abs(traces_ref[1]), axis=0, keepdims=True),
    )
    peak_ref[...] = peak.astype(jnp.float32)


def of_core(core, beside, zone):
    each = core[0].shape[0]
    return core[beside * PARTS + zone // each][zone % each]


def sketch_kernel(held, peak_ref, stay_ref, near_ref, far_ref, *refs):
    core, pieces, out_ref = refs[: 2 * PARTS], refs[2 * PARTS : -1], refs[-1]
    count = out_ref.shape[-1] - 1
    zones, half = stay_ref.shape[0], near_ref.shape[0]
    totals = [None, None]
    for slot in range(0, GROUPS * zones, 2):
        beside, zone = slot % GROUPS // 2, slot // GROUPS
        if beside:
            own = near_ref[zone] if zone < half else far_ref[zone - half]
        else:
            own = stay_ref[zone]
        which, at = held[slot]
        for rows, data in enumerate((own, of_core(core, beside, zone))):
            term = lax.dot_general(
                data, pieces[which][at], (((1,), (1,)), ((), ())), preferred_element_type=jnp.float32
            )
            totals[rows] = term if totals[rows] is None else totals[rows] + term
    for part, total in enumerate(totals):
        rows = total.shape[0] // 2
        out_ref[part, 0, :, :count] = total[:rows, :count] - total[rows:, count:]
        out_ref[part, 1, :, :count] = total[:rows, count:] + total[rows:, :count]
    peak = jnp.max(peak_ref[...], axis=1, keepdims=True)
    out_ref[:, :, :, count:] = jnp.broadcast_to(peak[None, None], out_ref.shape[:3] + (1,))


def gram_kernel(part_ref, other_ref, own_ref, core_ref):
    count = part_ref.shape[-1] - 1
    rows = part_ref.shape[2]
    products = []
    for which, out_ref in enumerate((own_ref, core_ref)):
        real = (part_ref[which, 0] + other_ref[1 - which, 0])[:, :count]
        imag = (part_ref[which, 1] + other_ref[1 - which, 1])[:, :count]
        out_ref[count : count + rows, :count] = real
        out_ref[count + rows :, :count] = imag
        both = jnp.concatenate([real, imag], axis=1)
        products.append(exact(both, both, ((0,), (0,))))
    product = products[0] + products[1]
    gram_re = product[:count, :count] + product[count:, count:]
    gram_im = product[:count, count:] - product[count:, :count]
    row = lax.broadcasted_iota(jnp.int32, gram_re.shape, 0)
    column = lax.broadcasted_iota(jnp.int32, gram_re.shape, 1)
    own_ref[:count, :count] = jnp.where(row <= column, gram_re, gram_im)
    peak = part_ref[0, 0, :1, count:] + other_ref[0, 0, :1, count:]
    own_ref[:, count:] = jnp.broadcast_to(peak, (own_ref.shape[0], 1))


def eliminate(real, imag):
    count, width = real.shape
    lane = lax.broadcasted_iota(jnp.int32, (ROWS, width), 1)
    row = lax.broadcasted_iota(jnp.int32, (ROWS, width), 0)
    blocks = count // ROWS
    re = [real[ROWS * i : ROWS * (i + 1)] for i in range(blocks)]
    im = [imag[ROWS * i : ROWS * (i + 1)] for i in range(blocks)]
    for b in range(blocks):
        col_re, col_im = [], []
        for o in range(ROWS):
            k = ROWS * b + o
            col_re.append([jnp.broadcast_to(re[i][:, k : k + 1], (ROWS, width)) for i in range(b, blocks)])
            col_im.append([jnp.broadcast_to(im[i][:, k : k + 1], (ROWS, width)) for i in range(b, blocks)])
        for o in range(ROWS):
            hit = lane == ROWS * b + o
            scale = lax.rsqrt(col_re[o][0][o : o + 1])
            pivot_re = jnp.where(hit[:1], scale, re[b][o : o + 1] * scale)
            pivot_im = jnp.where(hit[:1], 0.0, im[b][o : o + 1] * scale)
            by_re = [v * scale for v in col_re[o]]
            by_im = [v * scale for v in col_im[o]]
            for j in range(o + 1, ROWS):
                x_re, x_im = by_re[0][j : j + 1], by_im[0][j : j + 1]
                for q in range(blocks - b):
                    col_re[j][q] = col_re[j][q] - (by_re[q] * x_re + by_im[q] * x_im)
                    col_im[j][q] = col_im[j][q] - (by_im[q] * x_re - by_re[q] * x_im)
            for q, i in enumerate(range(b, blocks)):
                new_re = jnp.where(hit, 0.0, re[i]) - (by_re[q] * pivot_re - by_im[q] * pivot_im)
                new_im = jnp.where(hit, 0.0, im[i]) - (by_re[q] * pivot_im + by_im[q] * pivot_re)
                if i == b:
                    new_re = jnp.where(row > o, new_re, jnp.where(row == o, pivot_re, re[i]))
                    new_im = jnp.where(row > o, new_im, jnp.where(row == o, pivot_im, im[i]))
                re[i], im[i] = new_re, new_im
    return jnp.concatenate(re, axis=0), jnp.concatenate(im, axis=0)


def basis_kernel(scale, *refs):
    sketched, gram_ref, basis_ref, weights = refs[:GROUPS], refs[GROUPS], refs[GROUPS + 1], refs[GROUPS + 2 :]
    count = gram_ref.shape[0]
    rows = basis_ref.shape[1]
    packed = gram_ref[:, :count]
    flipped = packed.T
    row = lax.broadcasted_iota(jnp.int32, packed.shape, 0)
    column = lax.broadcasted_iota(jnp.int32, packed.shape, 1)
    gram_re = jnp.where(row <= column, packed, flipped)
    gram_im = jnp.where(row > column, packed, jnp.where(row < column, -flipped, 0.0))
    low_re, low_im = eliminate(gram_re, gram_im)
    low_re = jnp.where(row >= column, low_re, 0.0)
    low_im = jnp.where(row >= column, low_im, 0.0)
    stacked = jnp.concatenate([ref[count:, :count] for ref in sketched], axis=0)
    by_re = exact(stacked, low_re, ((1,), (1,)))
    by_im = exact(stacked, low_im, ((1,), (1,)))
    for group in range(GROUPS):
        real = slice(2 * rows * group, 2 * rows * group + rows)
        imag = slice(2 * rows * group + rows, 2 * rows * (group + 1))
        ortho_re = by_re[real] + by_im[imag]
        ortho_im = by_re[imag] - by_im[real]
        if group == 0:
            basis_ref[0] = ortho_re * scale
            basis_ref[1] = ortho_im * scale
        flat_re, flat_im = ortho_re.T, ortho_im.T
        top = jnp.concatenate([flat_re, flat_im], axis=1)
        low = jnp.concatenate([-flat_im, flat_re], axis=1)
        weights[group][...] = jnp.concatenate([top, low], axis=0).astype(jnp.bfloat16)


def project_kernel(bound, gram_ref, *refs):
    weights, (stay_ref, near_ref, far_ref, cross_ref) = refs[:GROUPS], refs[GROUPS : GROUPS + 4]
    core, (own_ref, side_ref, *far_outs) = refs[GROUPS + 4 : GROUPS + 4 + 2 * PARTS], refs[GROUPS + 4 + 2 * PARTS :]
    count = gram_ref.shape[0]
    factor = TOP / (gram_ref[:1, count : count + 1] * bound)
    half = near_ref.shape[0]

    def project(*data):
        total = None
        for weight_ref, block in zip(weights, data):
            term = jnp.dot(weight_ref[...], block, preferred_element_type=jnp.float32)
            total = term if total is None else total + term
        return total * factor

    for zone in range(half):
        far_outs[zone][...] = project(
            stay_ref[half + zone], of_core(core, 0, half + zone), far_ref[zone], cross_ref[zone]
        )
    for zone in range(half):
        side_ref[zone] = project(near_ref[zone], of_core(core, 1, zone))
        own_ref[zone] = project(stay_ref[zone], of_core(core, 0, zone))


def tied(first, second):
    first, second = list(first), list(second)
    both = lax.optimization_barrier(tuple(first + second))
    return list(both[: len(first)]), list(both[len(first) :])


def gather_slots(piece, size, ahead):
    bits = size.bit_length() - 1
    direct = min(bits, 4)
    have = {0: piece}
    for level in range(1, direct):
        if level == 2:
            (have[1 << direct - 1],), _ = tied([have[1 << direct - 1]], [ahead])
        for slot in range(0, 1 << direct, 2):
            if slot.bit_count() == level:
                along = slot & -slot if slot >> direct - 1 else 1 << slot.bit_length() - 1
                have[slot] = swap(have[slot ^ along], along, size)
    pieces = [(have[slot], [slot]) for slot in sorted(have, key=lambda slot: (slot.bit_count(), slot))]
    for bit in range(4, bits):
        whole = jnp.concatenate([value for value, _ in pieces])
        slots = [slot for _, held in pieces for slot in held]
        pieces = [(whole, slots), (swap(whole, 1 << bit, size), [slot | 1 << bit for slot in slots])]
    return pieces


def per_device(traces, sketch):
    size = lax.axis_size("rcv")
    me = lax.axis_index("rcv")
    rows, sources = traces.shape[1:]
    count, share = sketch.shape[1:]
    zones = size // GROUPS
    half = zones // 2
    bits = size.bit_length() - 1
    chunk = lambda slots: jax.ShapeDtypeStruct((slots, 2 * rows, share), traces.dtype)

    stay, near, far, cross, peak, *core = pl.pallas_call(
        functools.partial(chunk_kernel, share),
        out_shape=(
            chunk(zones),
            chunk(half),
            chunk(half),
            chunk(half),
            jax.ShapeDtypeStruct((1, sources), jnp.float32),
        )
        + (chunk(zones // PARTS),) * (2 * PARTS),
        in_specs=[SMEM, VMEM],
        out_specs=(VMEM,) * (5 + 2 * PARTS),
        scratch_shapes=[pltpu.VMEM((GROUPS, zones, 2 * rows, share), traces.dtype)],
        compiler_params=PARAMS,
        name="source_chunks",
    )(me.astype(jnp.int32).reshape(1), traces)
    core_in = [swap(value, 1, size) for value in core]
    pieces = gather_slots(sketch.reshape(1, 2 * count, share), size, stay)
    values = [value for value, _ in pieces]
    held = {slot: (which, at) for which, (_, slots) in enumerate(pieces) for at, slot in enumerate(slots)}
    partial = pl.pallas_call(
        functools.partial(sketch_kernel, held),
        out_shape=jax.ShapeDtypeStruct((2, 2, rows, count + 1), jnp.float32),
        in_specs=[VMEM] * (4 + 2 * PARTS + len(values)),
        out_specs=VMEM,
        compiler_params=PARAMS,
        name="sketch_rows",
    )(peak, stay, near, far, *core_in, *values)
    packet = jax.ShapeDtypeStruct((count + 2 * rows, count + 1), jnp.float32)
    own_packet, core_packet = pl.pallas_call(
        gram_kernel,
        out_shape=(packet, packet),
        in_specs=[VMEM] * 2,
        out_specs=(VMEM, VMEM),
        compiler_params=PARAMS,
        name="chip_gram",
    )(partial, swap(partial, 1, size))

    beside = swap(own_packet, 2, size)
    known = [own_packet, core_packet, beside, swap(beside, 1, size)]
    (far_out, cross_out), _ = tied([far, cross], [own_packet])
    far_in, cross_in = swap(far_out, 2, size), swap(cross_out, 3, size)
    gram = own_packet[:count] + beside[:count]
    for bit in range(2, bits):
        gram = gram + swap(gram, 1 << bit, size)

    basis, *weights = pl.pallas_call(
        functools.partial(basis_kernel, math.sqrt(rows * size)),
        out_shape=(jax.ShapeDtypeStruct((2, rows, count), jnp.float32),)
        + (jax.ShapeDtypeStruct((2 * count, 2 * rows), jnp.bfloat16),) * GROUPS,
        in_specs=[VMEM] * (1 + GROUPS),
        out_specs=(VMEM,) * (1 + GROUPS),
        compiler_params=PARAMS,
        cost_estimate=pl.CostEstimate(flops=1_500_000_000, bytes_accessed=1_000_000, transcendentals=0),
        name="orthonormal_basis",
    )(*known, gram)
    bound = 1.01 * math.sqrt(2 * rows * size)
    own, side, *away = pl.pallas_call(
        functools.partial(project_kernel, bound),
        out_shape=(
            jax.ShapeDtypeStruct((half, 2 * count, share), jnp.float32),
            jax.ShapeDtypeStruct((half, 2 * count, share), jnp.float32),
        )
        + (jax.ShapeDtypeStruct((2 * count, share), jnp.float32),) * half,
        in_specs=[VMEM] * (1 + GROUPS + 4 + 2 * PARTS),
        out_specs=(VMEM,) * (2 + half),
        compiler_params=PARAMS,
        name="project_rows",
    )(gram, *weights, stay, near, far_in, cross_in, *core_in)

    send = lambda value, mask: swap(value.astype(jnp.float16), mask, size).astype(jnp.float32)
    if zones <= 4:
        side = send(side, 2)
        parts = [send(away[zone], GROUPS * (half + zone)) for zone in reversed(range(half))]
        parts += [send(own[zone] + side[zone], GROUPS * zone) for zone in range(1, half)]
        total = own[0] + side[0] + sum(parts)
    else:
        total = own + send(side, 2) + send(jnp.stack(away), GROUPS * half)
        while total.shape[0] > 1:
            low, high = jnp.split(total, 2)
            total = low + send(high, GROUPS * low.shape[0])
        total = total[0]
    level = gram[0, count] * bound
    return basis, (total * (level / TOP)).reshape(2, count, share)


def solution(mesh):
    return jax.shard_map(
        per_device,
        mesh=mesh,
        in_specs=(P(None, ("grp", "rcv"), None), P(None, None, "rcv")),
        out_specs=(P(None, ("grp", "rcv"), None), P(None, "grp", "rcv")),
        check_vma=False,
    )
```

```python
import functools
import math

import jax
import jax.numpy as jnp
from jax import lax
from jax.experimental import pallas as pl
from jax.experimental.pallas import tpu as pltpu
from jax.sharding import PartitionSpec as P

ROWS = 8
GROUPS = 4
PARTS = 4
TOP = 32768.0
VMEM = pl.BlockSpec(memory_space=pltpu.VMEM)
SMEM = pl.BlockSpec(memory_space=pltpu.SMEM)
PARAMS = pltpu.CompilerParams(vmem_limit_bytes=40 * 1024 * 1024)


def swap(value, mask, size):
    return lax.ppermute(value, "rcv", [(i, i ^ mask) for i in range(size)])


def exact(left, right, dims):
    return lax.dot_general(
        left,
        right,
        ((dims[0], dims[1]), ((), ())),
        precision=lax.Precision.HIGHEST,
        preferred_element_type=jnp.float32,
    )


def chunk_kernel(share, me_ref, traces_ref, stay_ref, near_ref, far_ref, cross_ref, peak_ref, *refs):
    core, held_ref = refs[:-1], refs[-1]
    rows, sources = traces_ref.shape[1:]
    me = me_ref[0]
    for owner in range(sources // share):
        away = owner ^ me
        for part in range(2):
            held_ref[away % GROUPS, away // GROUPS, rows * part : rows * (part + 1), :] = traces_ref[
                part, :, owner * share : (owner + 1) * share
            ]
    zones, half = stay_ref.shape[0], near_ref.shape[0]
    for at, ref in enumerate(core):
        first = at % PARTS * ref.shape[0]
        ref[...] = held_ref[1 + at // PARTS * 2, first : first + ref.shape[0]]
    stay_ref[...] = held_ref[0]
    near_ref[...] = held_ref[2, :half]
    far_ref[...] = held_ref[2, half:]
    cross_ref[...] = held_ref[3, half:]
    peak = jnp.maximum(
        jnp.max(jnp.abs(traces_ref[0]), axis=0, keepdims=True),
        jnp.max(jnp.abs(traces_ref[1]), axis=0, keepdims=True),
    )
    peak_ref[...] = peak.astype(jnp.float32)


def of_core(core, beside, zone):
    each = core[0].shape[0]
    return core[beside * PARTS + zone // each][zone % each]


def sketch_kernel(held, peak_ref, stay_ref, near_ref, far_ref, *refs):
    core, pieces, out_ref = refs[: 2 * PARTS], refs[2 * PARTS : -1], refs[-1]
    count = out_ref.shape[-1] - 1
    zones, half = stay_ref.shape[0], near_ref.shape[0]
    totals = [None, None]
    for slot in range(0, GROUPS * zones, 2):
        beside, zone = slot % GROUPS // 2, slot // GROUPS
        if beside:
            own = near_ref[zone] if zone < half else far_ref[zone - half]
        else:
            own = stay_ref[zone]
        which, at = held[slot]
        for rows, data in enumerate((own, of_core(core, beside, zone))):
            term = lax.dot_general(
                data, pieces[which][at], (((1,), (1,)), ((), ())), preferred_element_type=jnp.float32
            )
            totals[rows] = term if totals[rows] is None else totals[rows] + term
    for part, total in enumerate(totals):
        rows = total.shape[0] // 2
        out_ref[part, 0, :, :count] = total[:rows, :count] - total[rows:, count:]
        out_ref[part, 1, :, :count] = total[:rows, count:] + total[rows:, :count]
    peak = jnp.max(peak_ref[...], axis=1, keepdims=True)
    out_ref[:, :, :, count:] = jnp.broadcast_to(peak[None, None], out_ref.shape[:3] + (1,))


def gram_kernel(part_ref, other_ref, own_ref, core_ref):
    count = part_ref.shape[-1] - 1
    rows = part_ref.shape[2]
    products = []
    for which, out_ref in enumerate((own_ref, core_ref)):
        real = (part_ref[which, 0] + other_ref[1 - which, 0])[:, :count]
        imag = (part_ref[which, 1] + other_ref[1 - which, 1])[:, :count]
        out_ref[count : count + rows, :count] = real
        out_ref[count + rows :, :count] = imag
        both = jnp.concatenate([real, imag], axis=1)
        products.append(exact(both, both, ((0,), (0,))))
    product = products[0] + products[1]
    gram_re = product[:count, :count] + product[count:, count:]
    gram_im = product[:count, count:] - product[count:, :count]
    row = lax.broadcasted_iota(jnp.int32, gram_re.shape, 0)
    column = lax.broadcasted_iota(jnp.int32, gram_re.shape, 1)
    own_ref[:count, :count] = jnp.where(row <= column, gram_re, gram_im)
    peak = part_ref[0, 0, :1, count:] + other_ref[0, 0, :1, count:]
    own_ref[:, count:] = jnp.broadcast_to(peak, (own_ref.shape[0], 1))


def eliminate(real, imag):
    count, width = real.shape
    lane = lax.broadcasted_iota(jnp.int32, (ROWS, width), 1)
    row = lax.broadcasted_iota(jnp.int32, (ROWS, width), 0)
    blocks = count // ROWS
    re = [real[ROWS * i : ROWS * (i + 1)] for i in range(blocks)]
    im = [imag[ROWS * i : ROWS * (i + 1)] for i in range(blocks)]
    for b in range(blocks):
        col_re, col_im = [], []
        for o in range(ROWS):
            k = ROWS * b + o
            col_re.append([jnp.broadcast_to(re[i][:, k : k + 1], (ROWS, width)) for i in range(b, blocks)])
            col_im.append([jnp.broadcast_to(im[i][:, k : k + 1], (ROWS, width)) for i in range(b, blocks)])
        for o in range(ROWS):
            hit = lane == ROWS * b + o
            scale = lax.rsqrt(col_re[o][0][o : o + 1])
            pivot_re = jnp.where(hit[:1], scale, re[b][o : o + 1] * scale)
            pivot_im = jnp.where(hit[:1], 0.0, im[b][o : o + 1] * scale)
            by_re = [v * scale for v in col_re[o]]
            by_im = [v * scale for v in col_im[o]]
            for j in range(o + 1, ROWS):
                x_re, x_im = by_re[0][j : j + 1], by_im[0][j : j + 1]
                for q in range(blocks - b):
                    col_re[j][q] = col_re[j][q] - (by_re[q] * x_re + by_im[q] * x_im)
                    col_im[j][q] = col_im[j][q] - (by_im[q] * x_re - by_re[q] * x_im)
            for q, i in enumerate(range(b, blocks)):
                new_re = jnp.where(hit, 0.0, re[i]) - (by_re[q] * pivot_re - by_im[q] * pivot_im)
                new_im = jnp.where(hit, 0.0, im[i]) - (by_re[q] * pivot_im + by_im[q] * pivot_re)
                if i == b:
                    new_re = jnp.where(row > o, new_re, jnp.where(row == o, pivot_re, re[i]))
                    new_im = jnp.where(row > o, new_im, jnp.where(row == o, pivot_im, im[i]))
                re[i], im[i] = new_re, new_im
    return jnp.concatenate(re, axis=0), jnp.concatenate(im, axis=0)


def basis_kernel(scale, *refs):
    sketched, gram_ref, basis_ref, weights = refs[:GROUPS], refs[GROUPS], refs[GROUPS + 1], refs[GROUPS + 2 :]
    count = gram_ref.shape[0]
    rows = basis_ref.shape[1]
    packed = gram_ref[:, :count]
    flipped = packed.T
    row = lax.broadcasted_iota(jnp.int32, packed.shape, 0)
    column = lax.broadcasted_iota(jnp.int32, packed.shape, 1)
    gram_re = jnp.where(row <= column, packed, flipped)
    gram_im = jnp.where(row > column, packed, jnp.where(row < column, -flipped, 0.0))
    low_re, low_im = eliminate(gram_re, gram_im)
    low_re = jnp.where(row >= column, low_re, 0.0)
    low_im = jnp.where(row >= column, low_im, 0.0)
    stacked = jnp.concatenate([ref[count:, :count] for ref in sketched], axis=0)
    by_re = exact(stacked, low_re, ((1,), (1,)))
    by_im = exact(stacked, low_im, ((1,), (1,)))
    for group in range(GROUPS):
        real = slice(2 * rows * group, 2 * rows * group + rows)
        imag = slice(2 * rows * group + rows, 2 * rows * (group + 1))
        ortho_re = by_re[real] + by_im[imag]
        ortho_im = by_re[imag] - by_im[real]
        if group == 0:
            basis_ref[0] = ortho_re * scale
            basis_ref[1] = ortho_im * scale
        flat_re, flat_im = ortho_re.T, ortho_im.T
        top = jnp.concatenate([flat_re, flat_im], axis=1)
        low = jnp.concatenate([-flat_im, flat_re], axis=1)
        weights[group][...] = jnp.concatenate([top, low], axis=0).astype(jnp.bfloat16)


def project_kernel(bound, gram_ref, *refs):
    weights, (stay_ref, near_ref, far_ref, cross_ref) = refs[:GROUPS], refs[GROUPS : GROUPS + 4]
    core, (own_ref, side_ref, *far_outs) = refs[GROUPS + 4 : GROUPS + 4 + 2 * PARTS], refs[GROUPS + 4 + 2 * PARTS :]
    count = gram_ref.shape[0]
    factor = TOP / (gram_ref[:1, count : count + 1] * bound)
    half = near_ref.shape[0]

    def project(*data):
        total = None
        for weight_ref, block in zip(weights, data):
            term = jnp.dot(weight_ref[...], block, preferred_element_type=jnp.float32)
            total = term if total is None else total + term
        return total * factor

    for zone in range(half):
        far_outs[zone][...] = project(
            stay_ref[half + zone], of_core(core, 0, half + zone), far_ref[zone], cross_ref[zone]
        )
    for zone in range(half):
        side_ref[zone] = project(near_ref[zone], of_core(core, 1, zone))
        own_ref[zone] = project(stay_ref[zone], of_core(core, 0, zone))


def tied(first, second):
    first, second = list(first), list(second)
    both = lax.optimization_barrier(tuple(first + second))
    return list(both[: len(first)]), list(both[len(first) :])


def gather_slots(piece, size, ahead):
    bits = size.bit_length() - 1
    direct = min(bits, 4)
    have = {0: piece}
    for level in range(1, direct):
        if level == 2:
            first = [1 << bit for bit in reversed(range(1, direct))]
            values, _ = tied([have[slot] for slot in first], [ahead])
            have.update(zip(first, values))
        for slot in range(0, 1 << direct, 2):
            if slot.bit_count() == level:
                along = slot & -slot if slot >> direct - 1 else 1 << slot.bit_length() - 1
                have[slot] = swap(have[slot ^ along], along, size)
    pieces = [(have[slot], [slot]) for slot in sorted(have, key=lambda slot: (slot.bit_count(), slot))]
    for bit in range(4, bits):
        whole = jnp.concatenate([value for value, _ in pieces])
        slots = [slot for _, held in pieces for slot in held]
        pieces = [(whole, slots), (swap(whole, 1 << bit, size), [slot | 1 << bit for slot in slots])]
    return pieces


def per_device(traces, sketch):
    size = lax.axis_size("rcv")
    me = lax.axis_index("rcv")
    rows, sources = traces.shape[1:]
    count, share = sketch.shape[1:]
    zones = size // GROUPS
    half = zones // 2
    bits = size.bit_length() - 1
    chunk = lambda slots: jax.ShapeDtypeStruct((slots, 2 * rows, share), traces.dtype)

    stay, near, far, cross, peak, *core = pl.pallas_call(
        functools.partial(chunk_kernel, share),
        out_shape=(
            chunk(zones),
            chunk(half),
            chunk(half),
            chunk(half),
            jax.ShapeDtypeStruct((1, sources), jnp.float32),
        )
        + (chunk(zones // PARTS),) * (2 * PARTS),
        in_specs=[SMEM, VMEM],
        out_specs=(VMEM,) * (5 + 2 * PARTS),
        scratch_shapes=[pltpu.VMEM((GROUPS, zones, 2 * rows, share), traces.dtype)],
        compiler_params=PARAMS,
        name="source_chunks",
    )(me.astype(jnp.int32).reshape(1), traces)
    core_in = [swap(value, 1, size) for value in core]
    pieces = gather_slots(sketch.reshape(1, 2 * count, share), size, stay)
    values = [value for value, _ in pieces]
    held = {slot: (which, at) for which, (_, slots) in enumerate(pieces) for at, slot in enumerate(slots)}
    partial = pl.pallas_call(
        functools.partial(sketch_kernel, held),
        out_shape=jax.ShapeDtypeStruct((2, 2, rows, count + 1), jnp.float32),
        in_specs=[VMEM] * (4 + 2 * PARTS + len(values)),
        out_specs=VMEM,
        compiler_params=PARAMS,
        name="sketch_rows",
    )(peak, stay, near, far, *core_in, *values)
    packet = jax.ShapeDtypeStruct((count + 2 * rows, count + 1), jnp.float32)
    own_packet, core_packet = pl.pallas_call(
        gram_kernel,
        out_shape=(packet, packet),
        in_specs=[VMEM] * 2,
        out_specs=(VMEM, VMEM),
        compiler_params=PARAMS,
        name="chip_gram",
    )(partial, swap(partial, 1, size))

    beside = swap(own_packet, 2, size)
    known = [own_packet, core_packet, beside, swap(beside, 1, size)]
    (far_out, cross_out), _ = tied([far, cross], [own_packet])
    far_in, cross_in = swap(far_out, 2, size), swap(cross_out, 3, size)
    gram = own_packet[:count] + beside[:count]
    for bit in range(2, bits):
        gram = gram + swap(gram, 1 << bit, size)

    basis, *weights = pl.pallas_call(
        functools.partial(basis_kernel, math.sqrt(rows * size)),
        out_shape=(jax.ShapeDtypeStruct((2, rows, count), jnp.float32),)
        + (jax.ShapeDtypeStruct((2 * count, 2 * rows), jnp.bfloat16),) * GROUPS,
        in_specs=[VMEM] * (1 + GROUPS),
        out_specs=(VMEM,) * (1 + GROUPS),
        compiler_params=PARAMS,
        cost_estimate=pl.CostEstimate(flops=1_500_000_000, bytes_accessed=1_000_000, transcendentals=0),
        name="orthonormal_basis",
    )(*known, gram)
    bound = 1.01 * math.sqrt(2 * rows * size)
    own, side, *away = pl.pallas_call(
        functools.partial(project_kernel, bound),
        out_shape=(
            jax.ShapeDtypeStruct((half, 2 * count, share), jnp.float32),
            jax.ShapeDtypeStruct((half, 2 * count, share), jnp.float32),
        )
        + (jax.ShapeDtypeStruct((2 * count, share), jnp.float32),) * half,
        in_specs=[VMEM] * (1 + GROUPS + 4 + 2 * PARTS),
        out_specs=(VMEM,) * (2 + half),
        compiler_params=PARAMS,
        name="project_rows",
    )(gram, *weights, stay, near, far_in, cross_in, *core_in)

    send = lambda value, mask: swap(value.astype(jnp.float16), mask, size).astype(jnp.float32)
    if zones <= 4:
        side = send(side, 2)
        parts = [send(away[zone], GROUPS * (half + zone)) for zone in reversed(range(half))]
        parts += [send(own[zone] + side[zone], GROUPS * zone) for zone in range(1, half)]
        total = own[0] + side[0] + sum(parts)
    else:
        total = own + send(side, 2) + send(jnp.stack(away), GROUPS * half)
        while total.shape[0] > 1:
            low, high = jnp.split(total, 2)
            total = low + send(high, GROUPS * low.shape[0])
        total = total[0]
    level = gram[0, count] * bound
    return basis, (total * (level / TOP)).reshape(2, count, share)


def solution(mesh):
    return jax.shard_map(
        per_device,
        mesh=mesh,
        in_specs=(P(None, ("grp", "rcv"), None), P(None, None, "rcv")),
        out_specs=(P(None, ("grp", "rcv"), None), P(None, "grp", "rcv")),
        check_vma=False,
    )
```

```python
import functools
import math

import jax
import jax.numpy as jnp
from jax import lax
from jax.experimental import pallas as pl
from jax.experimental.pallas import tpu as pltpu
from jax.sharding import PartitionSpec as P

ROWS = 8
GROUPS = 4
PARTS = 4
TOP = 32768.0
VMEM = pl.BlockSpec(memory_space=pltpu.VMEM)
SMEM = pl.BlockSpec(memory_space=pltpu.SMEM)
PARAMS = pltpu.CompilerParams(vmem_limit_bytes=40 * 1024 * 1024)


def swap(value, mask, size):
    return lax.ppermute(value, "rcv", [(i, i ^ mask) for i in range(size)])


def exact(left, right, dims):
    return lax.dot_general(
        left,
        right,
        ((dims[0], dims[1]), ((), ())),
        precision=lax.Precision.HIGHEST,
        preferred_element_type=jnp.float32,
    )


def chunk_kernel(share, me_ref, traces_ref, stay_ref, near_ref, far_ref, cross_ref, peak_ref, *refs):
    core, held_ref = refs[:-1], refs[-1]
    rows, sources = traces_ref.shape[1:]
    me = me_ref[0]
    for owner in range(sources // share):
        away = owner ^ me
        for part in range(2):
            held_ref[away % GROUPS, away // GROUPS, rows * part : rows * (part + 1), :] = traces_ref[
                part, :, owner * share : (owner + 1) * share
            ]
    zones, half = stay_ref.shape[0], near_ref.shape[0]
    for at, ref in enumerate(core):
        first = at % PARTS * ref.shape[0]
        ref[...] = held_ref[1 + at // PARTS * 2, first : first + ref.shape[0]]
    stay_ref[...] = held_ref[0]
    near_ref[...] = held_ref[2, :half]
    far_ref[...] = held_ref[2, half:]
    cross_ref[...] = held_ref[3, half:]
    peak = jnp.maximum(
        jnp.max(jnp.abs(traces_ref[0]), axis=0, keepdims=True),
        jnp.max(jnp.abs(traces_ref[1]), axis=0, keepdims=True),
    )
    peak_ref[...] = peak.astype(jnp.float32)


def of_core(core, beside, zone):
    each = core[0].shape[0]
    return core[beside * PARTS + zone // each][zone % each]


def sketch_kernel(held, peak_ref, stay_ref, near_ref, far_ref, *refs):
    core, pieces, out_ref = refs[: 2 * PARTS], refs[2 * PARTS : -1], refs[-1]
    count = out_ref.shape[-1] - 1
    zones, half = stay_ref.shape[0], near_ref.shape[0]
    totals = [None, None]
    for slot in range(0, GROUPS * zones, 2):
        beside, zone = slot % GROUPS // 2, slot // GROUPS
        if beside:
            own = near_ref[zone] if zone < half else far_ref[zone - half]
        else:
            own = stay_ref[zone]
        which, at = held[slot]
        for rows, data in enumerate((own, of_core(core, beside, zone))):
            term = lax.dot_general(
                data, pieces[which][at], (((1,), (1,)), ((), ())), preferred_element_type=jnp.float32
            )
            totals[rows] = term if totals[rows] is None else totals[rows] + term
    for part, total in enumerate(totals):
        rows = total.shape[0] // 2
        out_ref[part, 0, :, :count] = total[:rows, :count] - total[rows:, count:]
        out_ref[part, 1, :, :count] = total[:rows, count:] + total[rows:, :count]
    peak = jnp.max(peak_ref[...], axis=1, keepdims=True)
    out_ref[:, :, :, count:] = jnp.broadcast_to(peak[None, None], out_ref.shape[:3] + (1,))


def gram_kernel(part_ref, other_ref, own_ref, core_ref):
    count = part_ref.shape[-1] - 1
    rows = part_ref.shape[2]
    products = []
    for which, out_ref in enumerate((own_ref, core_ref)):
        real = (part_ref[which, 0] + other_ref[1 - which, 0])[:, :count]
        imag = (part_ref[which, 1] + other_ref[1 - which, 1])[:, :count]
        out_ref[count : count + rows, :count] = real
        out_ref[count + rows :, :count] = imag
        both = jnp.concatenate([real, imag], axis=1)
        products.append(exact(both, both, ((0,), (0,))))
    product = products[0] + products[1]
    gram_re = product[:count, :count] + product[count:, count:]
    gram_im = product[:count, count:] - product[count:, :count]
    row = lax.broadcasted_iota(jnp.int32, gram_re.shape, 0)
    column = lax.broadcasted_iota(jnp.int32, gram_re.shape, 1)
    own_ref[:count, :count] = jnp.where(row <= column, gram_re, gram_im)
    peak = part_ref[0, 0, :1, count:] + other_ref[0, 0, :1, count:]
    own_ref[:, count:] = jnp.broadcast_to(peak, (own_ref.shape[0], 1))


def eliminate(real, imag):
    count, width = real.shape
    lane = lax.broadcasted_iota(jnp.int32, (ROWS, width), 1)
    row = lax.broadcasted_iota(jnp.int32, (ROWS, width), 0)
    blocks = count // ROWS
    re = [real[ROWS * i : ROWS * (i + 1)] for i in range(blocks)]
    im = [imag[ROWS * i : ROWS * (i + 1)] for i in range(blocks)]
    out_re, out_im = [], []
    spread = lambda value: jnp.broadcast_to(value, (ROWS, width))
    pick = lambda value, at: spread(value[at : at + 1])
    solved = None
    for b in range(blocks):
        first = ROWS * b
        if b:
            old = first - ROWS
            cleared = (lane >= old) & (lane < first)
            next_re, next_im = jnp.where(cleared, 0.0, re[b]), jnp.where(cleared, 0.0, im[b])
            parts_re, parts_im = [], []
            for o in range(ROWS):
                c_re, c_im = spread(re[b][:, old + o : old + o + 1]), spread(im[b][:, old + o : old + o + 1])
                s_re, s_im = pick(solved[0], o), pick(solved[1], o)
                parts_re.append(c_re * s_re - c_im * s_im)
                parts_im.append(c_re * s_im + c_im * s_re)
            while len(parts_re) > 1:
                parts_re = [left + right for left, right in zip(parts_re[0::2], parts_re[1::2])]
                parts_im = [left + right for left, right in zip(parts_im[0::2], parts_im[1::2])]
            re[b], im[b] = next_re - parts_re[0], next_im - parts_im[0]
            if b + 1 < blocks:
                rest_re, rest_im = jnp.concatenate(re[b + 1 :]), jnp.concatenate(im[b + 1 :])
                columns = jnp.concatenate([rest_re[:, old:first], rest_im[:, old:first]], axis=1)
                weights = jnp.concatenate(
                    [
                        jnp.concatenate([solved[0], solved[1]], axis=1),
                        jnp.concatenate([-solved[1], solved[0]], axis=1),
                    ]
                )
                taken = exact(columns, weights, ((1,), (0,)))
                for at, i in enumerate(range(b + 1, blocks)):
                    some = slice(ROWS * at, ROWS * (at + 1))
                    re[i] = jnp.where(cleared, 0.0, re[i]) - taken[some, :width]
                    im[i] = jnp.where(cleared, 0.0, im[i]) - taken[some, width:]
        x_re, x_im = re[b], im[b]
        done_re, done_im = x_re, x_im
        col_re = [spread(x_re[:, first + o : first + o + 1]) for o in range(ROWS)]
        col_im = [spread(x_im[:, first + o : first + o + 1]) for o in range(ROWS)]
        live_re, live_im = list(col_re), list(col_im)
        for o in range(0, ROWS, 2):
            hit0, hit1 = lane == first + o, lane == first + o + 1
            hit = hit0 | hit1
            row0 = row == o
            pair = row0 | (row == o + 1)
            a, c = pick(live_re[o], o), pick(live_re[o + 1], o + 1)
            f_re, f_im = pick(live_re[o], o + 1), pick(live_im[o], o + 1)
            root = lax.rsqrt(a * c - (f_re * f_re + f_im * f_im))
            inverse = root * root

            def solve(re0, im0, re1, im1):
                return (
                    c * re0 - (f_re * re1 + f_im * im1),
                    c * im0 - (f_re * im1 - f_im * re1),
                    a * re1 - (f_re * re0 - f_im * im0),
                    a * im1 - (f_re * im0 + f_im * re0),
                )

            def less(z0_re, z0_im, z1_re, z1_im):
                return (
                    (col_re[o] * z0_re - col_im[o] * z0_im) + (col_re[o + 1] * z1_re - col_im[o + 1] * z1_im),
                    (col_re[o] * z0_im + col_im[o] * z0_re) + (col_re[o + 1] * z1_im + col_im[o + 1] * z1_re),
                )

            for j in range(o + 2, ROWS):
                z = solve(pick(live_re[j], o), pick(live_im[j], o), pick(live_re[j], o + 1), pick(live_im[j], o + 1))
                off_re, off_im = less(*z)
                live_re[j] = col_re[j] - off_re * inverse
                live_im[j] = col_im[j] - off_im * inverse
                col_re[j] = jnp.where(pair, jnp.where(row0, z[0], z[2]) * inverse, live_re[j])
                col_im[j] = jnp.where(pair, jnp.where(row0, z[1], z[3]) * inverse, live_im[j])
            re0 = jnp.where(hit0, 1.0, jnp.where(hit1, 0.0, pick(x_re, o)))
            re1 = jnp.where(hit1, 1.0, jnp.where(hit0, 0.0, pick(x_re, o + 1)))
            im0, im1 = jnp.where(hit, 0.0, pick(x_im, o)), jnp.where(hit, 0.0, pick(x_im, o + 1))
            z = solve(re0, im0, re1, im1)
            scale0 = lax.rsqrt(a)
            scale1 = root * scale0
            done_re = jnp.where(row0, re0 * scale0, jnp.where(pair, z[2] * scale1, done_re))
            done_im = jnp.where(row0, im0 * scale0, jnp.where(pair, z[3] * scale1, done_im))
            off_re, off_im = less(*z)
            x_re = jnp.where(
                pair, jnp.where(row0, z[0], z[2]) * inverse, jnp.where(hit, 0.0, x_re) - off_re * inverse
            )
            x_im = jnp.where(
                pair, jnp.where(row0, z[1], z[3]) * inverse, jnp.where(hit, 0.0, x_im) - off_im * inverse
            )
        out_re.append(done_re)
        out_im.append(done_im)
        solved = (x_re, x_im)
    return jnp.concatenate(out_re), jnp.concatenate(out_im)


def basis_kernel(scale, *refs):
    sketched, gram_ref, basis_ref, weights = refs[:GROUPS], refs[GROUPS], refs[GROUPS + 1], refs[GROUPS + 2 :]
    count = gram_ref.shape[0]
    rows = basis_ref.shape[1]
    packed = gram_ref[:, :count]
    flipped = packed.T
    row = lax.broadcasted_iota(jnp.int32, packed.shape, 0)
    column = lax.broadcasted_iota(jnp.int32, packed.shape, 1)
    gram_re = jnp.where(row <= column, packed, flipped)
    gram_im = jnp.where(row > column, packed, jnp.where(row < column, -flipped, 0.0))
    diagonal = jnp.where(row == column, gram_re, 0.0)
    across = lax.rsqrt(jnp.sum(diagonal, axis=0, keepdims=True))
    down = lax.rsqrt(jnp.sum(diagonal, axis=1, keepdims=True))
    padding = [(0, 0), (0, -count % 128)]
    low_re, low_im = eliminate(
        jnp.pad(gram_re * down * across, padding), jnp.pad(gram_im * down * across, padding)
    )
    low_re = jnp.where(row >= column, low_re[:, :count] * across, 0.0)
    low_im = jnp.where(row >= column, low_im[:, :count] * across, 0.0)
    stacked = jnp.concatenate([ref[count:, :count] for ref in sketched], axis=0)
    by_re = exact(stacked, low_re, ((1,), (1,)))
    by_im = exact(stacked, low_im, ((1,), (1,)))
    for group in range(GROUPS):
        real = slice(2 * rows * group, 2 * rows * group + rows)
        imag = slice(2 * rows * group + rows, 2 * rows * (group + 1))
        ortho_re = by_re[real] + by_im[imag]
        ortho_im = by_re[imag] - by_im[real]
        if group == 0:
            basis_ref[0] = ortho_re * scale
            basis_ref[1] = ortho_im * scale
        flat_re, flat_im = ortho_re.T, ortho_im.T
        top = jnp.concatenate([flat_re, flat_im], axis=1)
        low = jnp.concatenate([-flat_im, flat_re], axis=1)
        weights[group][...] = jnp.concatenate([top, low], axis=0).astype(jnp.bfloat16)


def project_kernel(bound, gram_ref, *refs):
    weights, (stay_ref, near_ref, far_ref, cross_ref) = refs[:GROUPS], refs[GROUPS : GROUPS + 4]
    core, (own_ref, side_ref, *far_outs) = refs[GROUPS + 4 : GROUPS + 4 + 2 * PARTS], refs[GROUPS + 4 + 2 * PARTS :]
    count = gram_ref.shape[0]
    factor = TOP / (gram_ref[:1, count : count + 1] * bound)
    half = near_ref.shape[0]

    def project(*data):
        total = None
        for weight_ref, block in zip(weights, data):
            term = jnp.dot(weight_ref[...], block, preferred_element_type=jnp.float32)
            total = term if total is None else total + term
        return total * factor

    for zone in range(half):
        far_outs[zone][...] = project(
            stay_ref[half + zone], of_core(core, 0, half + zone), far_ref[zone], cross_ref[zone]
        )
    for zone in range(half):
        side_ref[zone] = project(near_ref[zone], of_core(core, 1, zone))
        own_ref[zone] = project(stay_ref[zone], of_core(core, 0, zone))


def tied(first, second):
    first, second = list(first), list(second)
    both = lax.optimization_barrier(tuple(first + second))
    return list(both[: len(first)]), list(both[len(first) :])


def gather_slots(piece, size, ahead):
    bits = size.bit_length() - 1
    direct = min(bits, 4)
    have = {0: piece}
    for level in range(1, direct):
        if level == 2:
            first = [1 << bit for bit in reversed(range(1, direct))]
            values, _ = tied([have[slot] for slot in first], [ahead])
            have.update(zip(first, values))
        for slot in range(0, 1 << direct, 2):
            if slot.bit_count() == level:
                along = slot & -slot if slot >> direct - 1 else 1 << slot.bit_length() - 1
                have[slot] = swap(have[slot ^ along], along, size)
    pieces = [(have[slot], [slot]) for slot in sorted(have, key=lambda slot: (slot.bit_count(), slot))]
    for bit in range(4, bits):
        whole = jnp.concatenate([value for value, _ in pieces])
        slots = [slot for _, held in pieces for slot in held]
        pieces = [(whole, slots), (swap(whole, 1 << bit, size), [slot | 1 << bit for slot in slots])]
    return pieces


def per_device(traces, sketch):
    size = lax.axis_size("rcv")
    me = lax.axis_index("rcv")
    rows, sources = traces.shape[1:]
    count, share = sketch.shape[1:]
    zones = size // GROUPS
    half = zones // 2
    bits = size.bit_length() - 1
    chunk = lambda slots: jax.ShapeDtypeStruct((slots, 2 * rows, share), traces.dtype)

    stay, near, far, cross, peak, *core = pl.pallas_call(
        functools.partial(chunk_kernel, share),
        out_shape=(
            chunk(zones),
            chunk(half),
            chunk(half),
            chunk(half),
            jax.ShapeDtypeStruct((1, sources), jnp.float32),
        )
        + (chunk(zones // PARTS),) * (2 * PARTS),
        in_specs=[SMEM, VMEM],
        out_specs=(VMEM,) * (5 + 2 * PARTS),
        scratch_shapes=[pltpu.VMEM((GROUPS, zones, 2 * rows, share), traces.dtype)],
        compiler_params=PARAMS,
        name="source_chunks",
    )(me.astype(jnp.int32).reshape(1), traces)
    core_in = [swap(value, 1, size) for value in core]
    pieces = gather_slots(sketch.reshape(1, 2 * count, share), size, stay)
    values = [value for value, _ in pieces]
    held = {slot: (which, at) for which, (_, slots) in enumerate(pieces) for at, slot in enumerate(slots)}
    partial = pl.pallas_call(
        functools.partial(sketch_kernel, held),
        out_shape=jax.ShapeDtypeStruct((2, 2, rows, count + 1), jnp.float32),
        in_specs=[VMEM] * (4 + 2 * PARTS + len(values)),
        out_specs=VMEM,
        compiler_params=PARAMS,
        name="sketch_rows",
    )(peak, stay, near, far, *core_in, *values)
    packet = jax.ShapeDtypeStruct((count + 2 * rows, count + 1), jnp.float32)
    own_packet, core_packet = pl.pallas_call(
        gram_kernel,
        out_shape=(packet, packet),
        in_specs=[VMEM] * 2,
        out_specs=(VMEM, VMEM),
        compiler_params=PARAMS,
        name="chip_gram",
    )(partial, swap(partial, 1, size))

    beside = swap(own_packet, 2, size)
    known = [own_packet, core_packet, beside, swap(beside, 1, size)]
    (far_out, cross_out), _ = tied([far, cross], [own_packet])
    far_in, cross_in = swap(far_out, 2, size), swap(cross_out, 3, size)
    gram = own_packet[:count] + beside[:count]
    for bit in range(2, bits):
        gram = gram + swap(gram, 1 << bit, size)

    basis, *weights = pl.pallas_call(
        functools.partial(basis_kernel, math.sqrt(rows * size)),
        out_shape=(jax.ShapeDtypeStruct((2, rows, count), jnp.float32),)
        + (jax.ShapeDtypeStruct((2 * count, 2 * rows), jnp.bfloat16),) * GROUPS,
        in_specs=[VMEM] * (1 + GROUPS),
        out_specs=(VMEM,) * (1 + GROUPS),
        compiler_params=PARAMS,
        cost_estimate=pl.CostEstimate(flops=1_500_000_000, bytes_accessed=1_000_000, transcendentals=0),
        name="orthonormal_basis",
    )(*known, gram)
    bound = 1.01 * math.sqrt(2 * rows * size)
    own, side, *away = pl.pallas_call(
        functools.partial(project_kernel, bound),
        out_shape=(
            jax.ShapeDtypeStruct((half, 2 * count, share), jnp.float32),
            jax.ShapeDtypeStruct((half, 2 * count, share), jnp.float32),
        )
        + (jax.ShapeDtypeStruct((2 * count, share), jnp.float32),) * half,
        in_specs=[VMEM] * (1 + GROUPS + 4 + 2 * PARTS),
        out_specs=(VMEM,) * (2 + half),
        compiler_params=PARAMS,
        name="project_rows",
    )(gram, *weights, stay, near, far_in, cross_in, *core_in)

    send = lambda value, mask: swap(value.astype(jnp.float16), mask, size).astype(jnp.float32)
    if zones <= 4:
        side = send(side, 2)
        parts = [send(away[zone], GROUPS * (half + zone)) for zone in reversed(range(half))]
        parts += [send(own[zone] + side[zone], GROUPS * zone) for zone in range(1, half)]
        total = own[0] + side[0] + sum(parts)
    else:
        total = own + send(side, 2) + send(jnp.stack(away), GROUPS * half)
        while total.shape[0] > 1:
            low, high = jnp.split(total, 2)
            total = low + send(high, GROUPS * low.shape[0])
        total = total[0]
    level = gram[0, count] * bound
    return basis, (total * (level / TOP)).reshape(2, count, share)


def solution(mesh):
    return jax.shard_map(
        per_device,
        mesh=mesh,
        in_specs=(P(None, ("grp", "rcv"), None), P(None, None, "rcv")),
        out_specs=(P(None, ("grp", "rcv"), None), P(None, "grp", "rcv")),
        check_vma=False,
    )
```

```python
import functools
import math

import jax
import jax.numpy as jnp
from jax import lax
from jax.experimental import pallas as pl
from jax.experimental.pallas import tpu as pltpu
from jax.sharding import PartitionSpec as P

ROWS = 8
GROUPS = 4
PARTS = 2
TOP = 32768.0
VMEM = pl.BlockSpec(memory_space=pltpu.VMEM)
SMEM = pl.BlockSpec(memory_space=pltpu.SMEM)
PARAMS = pltpu.CompilerParams(vmem_limit_bytes=40 * 1024 * 1024)


def swap(value, mask, size):
    return lax.ppermute(value, "rcv", [(i, i ^ mask) for i in range(size)])


def exact(left, right, dims):
    return lax.dot_general(
        left,
        right,
        ((dims[0], dims[1]), ((), ())),
        precision=lax.Precision.HIGHEST,
        preferred_element_type=jnp.float32,
    )


def chunk_kernel(share, me_ref, traces_ref, stay_ref, near_ref, far_ref, cross_ref, peak_ref, *refs):
    core, held_ref = refs[:-1], refs[-1]
    rows, sources = traces_ref.shape[1:]
    me = me_ref[0]
    for owner in range(sources // share):
        away = owner ^ me
        for part in range(2):
            held_ref[away % GROUPS, away // GROUPS, rows * part : rows * (part + 1), :] = traces_ref[
                part, :, owner * share : (owner + 1) * share
            ]
    zones, half = stay_ref.shape[0], near_ref.shape[0]
    for at, ref in enumerate(core):
        first = at % PARTS * ref.shape[0]
        ref[...] = held_ref[1 + at // PARTS * 2, first : first + ref.shape[0]]
    stay_ref[...] = held_ref[0]
    near_ref[...] = held_ref[2, :half]
    far_ref[...] = held_ref[2, half:]
    cross_ref[...] = held_ref[3, half:]
    peak = jnp.maximum(
        jnp.max(jnp.abs(traces_ref[0]), axis=0, keepdims=True),
        jnp.max(jnp.abs(traces_ref[1]), axis=0, keepdims=True),
    )
    peak_ref[...] = peak.astype(jnp.float32)


def of_core(core, beside, zone):
    each = core[0].shape[0]
    return core[beside * PARTS + zone // each][zone % each]


def sketch_kernel(held, peak_ref, stay_ref, near_ref, far_ref, *refs):
    core, pieces, out_ref = refs[: 2 * PARTS], refs[2 * PARTS : -1], refs[-1]
    count = out_ref.shape[-1] - 1
    zones, half = stay_ref.shape[0], near_ref.shape[0]
    totals = [None, None]
    for slot in range(0, GROUPS * zones, 2):
        beside, zone = slot % GROUPS // 2, slot // GROUPS
        if beside:
            own = near_ref[zone] if zone < half else far_ref[zone - half]
        else:
            own = stay_ref[zone]
        which, at = held[slot]
        for rows, data in enumerate((own, of_core(core, beside, zone))):
            term = lax.dot_general(
                data, pieces[which][at], (((1,), (1,)), ((), ())), preferred_element_type=jnp.float32
            )
            totals[rows] = term if totals[rows] is None else totals[rows] + term
    for part, total in enumerate(totals):
        rows = total.shape[0] // 2
        out_ref[part, 0, :, :count] = total[:rows, :count] - total[rows:, count:]
        out_ref[part, 1, :, :count] = total[:rows, count:] + total[rows:, :count]
    peak = jnp.max(peak_ref[...], axis=1, keepdims=True)
    out_ref[:, :, :, count:] = jnp.broadcast_to(peak[None, None], out_ref.shape[:3] + (1,))


def gram_kernel(part_ref, other_ref, own_ref, core_ref):
    count = part_ref.shape[-1] - 1
    rows = part_ref.shape[2]
    products = []
    for which, out_ref in enumerate((own_ref, core_ref)):
        real = (part_ref[which, 0] + other_ref[1 - which, 0])[:, :count]
        imag = (part_ref[which, 1] + other_ref[1 - which, 1])[:, :count]
        out_ref[count : count + rows, :count] = real
        out_ref[count + rows :, :count] = imag
        both = jnp.concatenate([real, imag], axis=1)
        products.append(exact(both, both, ((0,), (0,))))
    product = products[0] + products[1]
    gram_re = product[:count, :count] + product[count:, count:]
    gram_im = product[:count, count:] - product[count:, :count]
    row = lax.broadcasted_iota(jnp.int32, gram_re.shape, 0)
    column = lax.broadcasted_iota(jnp.int32, gram_re.shape, 1)
    own_ref[:count, :count] = jnp.where(row <= column, gram_re, gram_im)
    peak = part_ref[0, 0, :1, count:] + other_ref[0, 0, :1, count:]
    own_ref[:, count:] = jnp.broadcast_to(peak, (own_ref.shape[0], 1))


def eliminate(real, imag):
    count, width = real.shape
    lane = lax.broadcasted_iota(jnp.int32, (ROWS, width), 1)
    row = lax.broadcasted_iota(jnp.int32, (ROWS, width), 0)
    blocks = count // ROWS
    re = [real[ROWS * i : ROWS * (i + 1)] for i in range(blocks)]
    im = [imag[ROWS * i : ROWS * (i + 1)] for i in range(blocks)]
    out_re, out_im = [], []
    spread = lambda value: jnp.broadcast_to(value, (ROWS, width))
    pick = lambda value, at: spread(value[at : at + 1])
    solved = None
    for b in range(blocks):
        first = ROWS * b
        if b:
            old = first - ROWS
            cleared = (lane >= old) & (lane < first)
            next_re, next_im = jnp.where(cleared, 0.0, re[b]), jnp.where(cleared, 0.0, im[b])
            parts_re, parts_im = [], []
            for o in range(ROWS):
                c_re, c_im = spread(re[b][:, old + o : old + o + 1]), spread(im[b][:, old + o : old + o + 1])
                s_re, s_im = pick(solved[0], o), pick(solved[1], o)
                parts_re.append(c_re * s_re - c_im * s_im)
                parts_im.append(c_re * s_im + c_im * s_re)
            while len(parts_re) > 1:
                parts_re = [left + right for left, right in zip(parts_re[0::2], parts_re[1::2])]
                parts_im = [left + right for left, right in zip(parts_im[0::2], parts_im[1::2])]
            re[b], im[b] = next_re - parts_re[0], next_im - parts_im[0]
            if b + 1 < blocks:
                rest_re, rest_im = jnp.concatenate(re[b + 1 :]), jnp.concatenate(im[b + 1 :])
                columns = jnp.concatenate([rest_re[:, old:first], rest_im[:, old:first]], axis=1)
                weights = jnp.concatenate(
                    [
                        jnp.concatenate([solved[0], solved[1]], axis=1),
                        jnp.concatenate([-solved[1], solved[0]], axis=1),
                    ]
                )
                taken = exact(columns, weights, ((1,), (0,)))
                for at, i in enumerate(range(b + 1, blocks)):
                    some = slice(ROWS * at, ROWS * (at + 1))
                    re[i] = jnp.where(cleared, 0.0, re[i]) - taken[some, :width]
                    im[i] = jnp.where(cleared, 0.0, im[i]) - taken[some, width:]
        x_re, x_im = re[b], im[b]
        done_re, done_im = x_re, x_im
        col_re = [spread(x_re[:, first + o : first + o + 1]) for o in range(ROWS)]
        col_im = [spread(x_im[:, first + o : first + o + 1]) for o in range(ROWS)]
        live_re, live_im = list(col_re), list(col_im)
        for o in range(0, ROWS, 2):
            hit0, hit1 = lane == first + o, lane == first + o + 1
            hit = hit0 | hit1
            row0 = row == o
            pair = row0 | (row == o + 1)
            a, c = pick(live_re[o], o), pick(live_re[o + 1], o + 1)
            f_re, f_im = pick(live_re[o], o + 1), pick(live_im[o], o + 1)
            root = lax.rsqrt(a * c - (f_re * f_re + f_im * f_im))
            inverse = root * root

            def solve(re0, im0, re1, im1):
                return (
                    c * re0 - (f_re * re1 + f_im * im1),
                    c * im0 - (f_re * im1 - f_im * re1),
                    a * re1 - (f_re * re0 - f_im * im0),
                    a * im1 - (f_re * im0 + f_im * re0),
                )

            def less(z0_re, z0_im, z1_re, z1_im):
                return (
                    (col_re[o] * z0_re - col_im[o] * z0_im) + (col_re[o + 1] * z1_re - col_im[o + 1] * z1_im),
                    (col_re[o] * z0_im + col_im[o] * z0_re) + (col_re[o + 1] * z1_im + col_im[o + 1] * z1_re),
                )

            for j in range(o + 2, ROWS):
                z = solve(pick(live_re[j], o), pick(live_im[j], o), pick(live_re[j], o + 1), pick(live_im[j], o + 1))
                off_re, off_im = less(*z)
                live_re[j] = col_re[j] - off_re * inverse
                live_im[j] = col_im[j] - off_im * inverse
                col_re[j] = jnp.where(pair, jnp.where(row0, z[0], z[2]) * inverse, live_re[j])
                col_im[j] = jnp.where(pair, jnp.where(row0, z[1], z[3]) * inverse, live_im[j])
            re0 = jnp.where(hit0, 1.0, jnp.where(hit1, 0.0, pick(x_re, o)))
            re1 = jnp.where(hit1, 1.0, jnp.where(hit0, 0.0, pick(x_re, o + 1)))
            im0, im1 = jnp.where(hit, 0.0, pick(x_im, o)), jnp.where(hit, 0.0, pick(x_im, o + 1))
            z = solve(re0, im0, re1, im1)
            scale0 = lax.rsqrt(a)
            scale1 = root * scale0
            done_re = jnp.where(row0, re0 * scale0, jnp.where(pair, z[2] * scale1, done_re))
            done_im = jnp.where(row0, im0 * scale0, jnp.where(pair, z[3] * scale1, done_im))
            off_re, off_im = less(*z)
            x_re = jnp.where(
                pair, jnp.where(row0, z[0], z[2]) * inverse, jnp.where(hit, 0.0, x_re) - off_re * inverse
            )
            x_im = jnp.where(
                pair, jnp.where(row0, z[1], z[3]) * inverse, jnp.where(hit, 0.0, x_im) - off_im * inverse
            )
        out_re.append(done_re)
        out_im.append(done_im)
        solved = (x_re, x_im)
    return jnp.concatenate(out_re), jnp.concatenate(out_im)


def basis_kernel(scale, *refs):
    sketched, gram_ref, basis_ref, weights = refs[:GROUPS], refs[GROUPS], refs[GROUPS + 1], refs[GROUPS + 2 :]
    count = gram_ref.shape[0]
    rows = basis_ref.shape[1]
    packed = gram_ref[:, :count]
    flipped = packed.T
    row = lax.broadcasted_iota(jnp.int32, packed.shape, 0)
    column = lax.broadcasted_iota(jnp.int32, packed.shape, 1)
    gram_re = jnp.where(row <= column, packed, flipped)
    gram_im = jnp.where(row > column, packed, jnp.where(row < column, -flipped, 0.0))
    diagonal = jnp.where(row == column, gram_re, 0.0)
    across = lax.rsqrt(jnp.sum(diagonal, axis=0, keepdims=True))
    down = lax.rsqrt(jnp.sum(diagonal, axis=1, keepdims=True))
    padding = [(0, 0), (0, -count % 128)]
    low_re, low_im = eliminate(
        jnp.pad(gram_re * down * across, padding), jnp.pad(gram_im * down * across, padding)
    )
    low_re = jnp.where(row >= column, low_re[:, :count] * across, 0.0)
    low_im = jnp.where(row >= column, low_im[:, :count] * across, 0.0)
    stacked = jnp.concatenate([ref[count:, :count] for ref in sketched], axis=0)
    by_re = exact(stacked, low_re, ((1,), (1,)))
    by_im = exact(stacked, low_im, ((1,), (1,)))
    for group in range(GROUPS):
        real = slice(2 * rows * group, 2 * rows * group + rows)
        imag = slice(2 * rows * group + rows, 2 * rows * (group + 1))
        ortho_re = by_re[real] + by_im[imag]
        ortho_im = by_re[imag] - by_im[real]
        if group == 0:
            basis_ref[0] = ortho_re * scale
            basis_ref[1] = ortho_im * scale
        flat_re, flat_im = ortho_re.T, ortho_im.T
        top = jnp.concatenate([flat_re, flat_im], axis=1)
        low = jnp.concatenate([-flat_im, flat_re], axis=1)
        weights[group][...] = jnp.concatenate([top, low], axis=0).astype(jnp.bfloat16)


def folds(rows, share):
    whole = share // 128 * 128
    rest = share - whole
    count = whole // rest if rest else 0
    return count if count and rows % (16 * count) == 0 else 0


def folded_shape(rows, share):
    count = folds(rows, share)
    return (rows + rows // count, share // 128 * 128) if count else (rows, share)


def fold(value):
    rows, share = value.shape
    count = folds(rows, share)
    if not count:
        return value
    whole, each = share // 128 * 128, rows // count
    rest = [value[each * i : each * (i + 1), whole:] for i in range(count)]
    spare = whole - count * (share - whole)
    if spare:
        rest.append(jnp.zeros((each, spare), value.dtype))
    return jnp.concatenate([value[:, :whole], jnp.concatenate(rest, axis=1)], axis=0)


def unfold_kernel(folded_ref, out_ref):
    rows, share = out_ref.shape
    count = folds(rows, share)
    if not count:
        out_ref[...] = folded_ref[...]
        return
    whole, each = share // 128 * 128, rows // count
    wide = share - whole
    out_ref[:, :whole] = folded_ref[:rows, :]
    for i in range(count):
        out_ref[each * i : each * (i + 1), whole:] = folded_ref[rows:, wide * i : wide * (i + 1)]


def project_kernel(bound, gram_ref, *refs):
    weights, (stay_ref, near_ref, far_ref, cross_ref) = refs[:GROUPS], refs[GROUPS : GROUPS + 4]
    core, (own_ref, side_ref, *far_outs) = refs[GROUPS + 4 : GROUPS + 4 + 2 * PARTS], refs[GROUPS + 4 + 2 * PARTS :]
    count = gram_ref.shape[0]
    factor = TOP / (gram_ref[:1, count : count + 1] * bound)
    half = near_ref.shape[0]

    def project(*data):
        total = None
        for weight_ref, block in zip(weights, data):
            term = jnp.dot(weight_ref[...], block, preferred_element_type=jnp.float32)
            total = term if total is None else total + term
        return fold(total * factor)

    for zone in range(half):
        far_outs[zone][...] = project(
            stay_ref[half + zone], of_core(core, 0, half + zone), far_ref[zone], cross_ref[zone]
        )
    for zone in range(half):
        side_ref[zone] = project(near_ref[zone], of_core(core, 1, zone))
        own_ref[zone] = project(stay_ref[zone], of_core(core, 0, zone))


def tied(first, second):
    first, second = list(first), list(second)
    both = lax.optimization_barrier(tuple(first + second))
    return list(both[: len(first)]), list(both[len(first) :])


def gather_slots(piece, size, ahead):
    bits = size.bit_length() - 1
    direct = min(bits, 4)
    have = {0: piece}
    for level in range(1, direct):
        if level == 2:
            first = [1 << bit for bit in reversed(range(1, direct))]
            values, _ = tied([have[slot] for slot in first], [ahead])
            have.update(zip(first, values))
        for slot in range(0, 1 << direct, 2):
            if slot.bit_count() == level:
                along = slot & -slot if slot >> direct - 1 else 1 << slot.bit_length() - 1
                have[slot] = swap(have[slot ^ along], along, size)
    pieces = [(have[slot], [slot]) for slot in sorted(have, key=lambda slot: (slot.bit_count(), slot))]
    for bit in range(4, bits):
        whole = jnp.concatenate([value for value, _ in pieces])
        slots = [slot for _, held in pieces for slot in held]
        pieces = [(whole, slots), (swap(whole, 1 << bit, size), [slot | 1 << bit for slot in slots])]
    return pieces


def per_device(traces, sketch):
    size = lax.axis_size("rcv")
    me = lax.axis_index("rcv")
    rows, sources = traces.shape[1:]
    count, share = sketch.shape[1:]
    zones = size // GROUPS
    half = zones // 2
    bits = size.bit_length() - 1
    chunk = lambda slots: jax.ShapeDtypeStruct((slots, 2 * rows, share), traces.dtype)

    stay, near, far, cross, peak, *core = pl.pallas_call(
        functools.partial(chunk_kernel, share),
        out_shape=(
            chunk(zones),
            chunk(half),
            chunk(half),
            chunk(half),
            jax.ShapeDtypeStruct((1, sources), jnp.float32),
        )
        + (chunk(zones // PARTS),) * (2 * PARTS),
        in_specs=[SMEM, VMEM],
        out_specs=(VMEM,) * (5 + 2 * PARTS),
        scratch_shapes=[pltpu.VMEM((GROUPS, zones, 2 * rows, share), traces.dtype)],
        compiler_params=PARAMS,
        name="source_chunks",
    )(me.astype(jnp.int32).reshape(1), traces)
    core_in = [swap(value, 1, size) for value in core]
    pieces = gather_slots(sketch.reshape(1, 2 * count, share), size, stay)
    values = [value for value, _ in pieces]
    held = {slot: (which, at) for which, (_, slots) in enumerate(pieces) for at, slot in enumerate(slots)}
    partial = pl.pallas_call(
        functools.partial(sketch_kernel, held),
        out_shape=jax.ShapeDtypeStruct((2, 2, rows, count + 1), jnp.float32),
        in_specs=[VMEM] * (4 + 2 * PARTS + len(values)),
        out_specs=VMEM,
        compiler_params=PARAMS,
        name="sketch_rows",
    )(peak, stay, near, far, *core_in, *values)
    packet = jax.ShapeDtypeStruct((count + 2 * rows, count + 1), jnp.float32)
    own_packet, core_packet = pl.pallas_call(
        gram_kernel,
        out_shape=(packet, packet),
        in_specs=[VMEM] * 2,
        out_specs=(VMEM, VMEM),
        compiler_params=PARAMS,
        name="chip_gram",
    )(partial, swap(partial, 1, size))

    beside = swap(own_packet, 2, size)
    known = [own_packet, core_packet, beside, swap(beside, 1, size)]
    (far_out, cross_out), _ = tied([far, cross], [own_packet])
    far_in, cross_in = swap(far_out, 2, size), swap(cross_out, 3, size)
    gram = own_packet[:count] + beside[:count]
    for bit in range(2, bits):
        gram = gram + swap(gram, 1 << bit, size)

    basis, *weights = pl.pallas_call(
        functools.partial(basis_kernel, math.sqrt(rows * size)),
        out_shape=(jax.ShapeDtypeStruct((2, rows, count), jnp.float32),)
        + (jax.ShapeDtypeStruct((2 * count, 2 * rows), jnp.bfloat16),) * GROUPS,
        in_specs=[VMEM] * (1 + GROUPS),
        out_specs=(VMEM,) * (1 + GROUPS),
        compiler_params=PARAMS,
        cost_estimate=pl.CostEstimate(flops=1_500_000_000, bytes_accessed=1_000_000, transcendentals=0),
        name="orthonormal_basis",
    )(*known, gram)
    folded = folded_shape(2 * count, share)
    bound = 1.01 * math.sqrt(2 * rows * size)
    own, side, *away = pl.pallas_call(
        functools.partial(project_kernel, bound),
        out_shape=(
            jax.ShapeDtypeStruct((half, *folded), jnp.float32),
            jax.ShapeDtypeStruct((half, *folded), jnp.float32),
        )
        + (jax.ShapeDtypeStruct(folded, jnp.float32),) * half,
        in_specs=[VMEM] * (1 + GROUPS + 4 + 2 * PARTS),
        out_specs=(VMEM,) * (2 + half),
        compiler_params=PARAMS,
        name="project_rows",
    )(gram, *weights, stay, near, far_in, cross_in, *core_in)

    send = lambda value, mask: swap(value.astype(jnp.float16), mask, size).astype(jnp.float32)
    if zones <= 4:
        side = send(side, 2)
        parts = [send(away[zone], GROUPS * (half + zone)) for zone in reversed(range(half))]
        parts += [send(own[zone] + side[zone], GROUPS * zone) for zone in range(1, half)]
        total = own[0] + side[0] + sum(parts)
    else:
        total = own + send(side, 2) + send(jnp.stack(away), GROUPS * half)
        while total.shape[0] > 1:
            low, high = jnp.split(total, 2)
            total = low + send(high, GROUPS * low.shape[0])
        total = total[0]
    level = gram[0, count] * bound
    total = total * (level / TOP)
    groups = folds(2 * count, share)
    if groups:
        rest = [total[2 * count :, i * (share - folded[1]) : (i + 1) * (share - folded[1])] for i in range(groups)]
        total = jnp.concatenate([total[: 2 * count], jnp.concatenate(rest)], axis=1)
    return basis, total.reshape(2, count, share)


def solution(mesh):
    return jax.shard_map(
        per_device,
        mesh=mesh,
        in_specs=(P(None, ("grp", "rcv"), None), P(None, None, "rcv")),
        out_specs=(P(None, ("grp", "rcv"), None), P(None, "grp", "rcv")),
        check_vma=False,
    )
```

```python
import functools
import math

import jax
import jax.numpy as jnp
from jax import lax
from jax.experimental import pallas as pl
from jax.experimental.pallas import tpu as pltpu
from jax.sharding import PartitionSpec as P

ROWS = 8
GROUPS = 4
PARTS = 2
TOP = 32768.0
VMEM = pl.BlockSpec(memory_space=pltpu.VMEM)
SMEM = pl.BlockSpec(memory_space=pltpu.SMEM)
PARAMS = pltpu.CompilerParams(vmem_limit_bytes=40 * 1024 * 1024)


def swap(value, mask, size):
    return lax.ppermute(value, "rcv", [(i, i ^ mask) for i in range(size)])


def exact(left, right, dims):
    return lax.dot_general(
        left,
        right,
        ((dims[0], dims[1]), ((), ())),
        precision=lax.Precision.HIGHEST,
        preferred_element_type=jnp.float32,
    )


def chunk_kernel(share, me_ref, traces_ref, stay_ref, near_ref, far_ref, cross_ref, peak_ref, *refs):
    core, held_ref = refs[:-1], refs[-1]
    rows, sources = traces_ref.shape[1:]
    me = me_ref[0]
    for owner in range(sources // share):
        away = owner ^ me
        for part in range(2):
            held_ref[away % GROUPS, away // GROUPS, rows * part : rows * (part + 1), :] = traces_ref[
                part, :, owner * share : (owner + 1) * share
            ]
    zones, half = stay_ref.shape[0], near_ref.shape[0]
    for at, ref in enumerate(core):
        first = at % PARTS * ref.shape[0]
        ref[...] = held_ref[1 + at // PARTS * 2, first : first + ref.shape[0]]
    stay_ref[...] = held_ref[0]
    near_ref[...] = held_ref[2, :half]
    far_ref[...] = held_ref[2, half:]
    cross_ref[...] = held_ref[3, half:]
    peak = jnp.maximum(
        jnp.max(jnp.abs(traces_ref[0]), axis=0, keepdims=True),
        jnp.max(jnp.abs(traces_ref[1]), axis=0, keepdims=True),
    )
    peak_ref[...] = peak.astype(jnp.float32)


def of_core(core, beside, zone):
    each = core[0].shape[0]
    return core[beside * PARTS + zone // each][zone % each]


def sketch_kernel(held, peak_ref, stay_ref, near_ref, far_ref, *refs):
    core, pieces, out_ref = refs[: 2 * PARTS], refs[2 * PARTS : -1], refs[-1]
    count = out_ref.shape[-1] - 1
    zones, half = stay_ref.shape[0], near_ref.shape[0]
    totals = [None, None]
    for slot in range(0, GROUPS * zones, 2):
        beside, zone = slot % GROUPS // 2, slot // GROUPS
        if beside:
            own = near_ref[zone] if zone < half else far_ref[zone - half]
        else:
            own = stay_ref[zone]
        which, at = held[slot]
        block = unfold(pieces[which][at], 2 * count, own.shape[1])
        for rows, data in enumerate((own, of_core(core, beside, zone))):
            term = lax.dot_general(data, block, (((1,), (1,)), ((), ())), preferred_element_type=jnp.float32)
            totals[rows] = term if totals[rows] is None else totals[rows] + term
    for part, total in enumerate(totals):
        rows = total.shape[0] // 2
        out_ref[part, 0, :, :count] = total[:rows, :count] - total[rows:, count:]
        out_ref[part, 1, :, :count] = total[:rows, count:] + total[rows:, :count]
    peak = jnp.max(peak_ref[...], axis=1, keepdims=True)
    out_ref[:, :, :, count:] = jnp.broadcast_to(peak[None, None], out_ref.shape[:3] + (1,))


def gram_kernel(part_ref, other_ref, own_ref, core_ref):
    count = part_ref.shape[-1] - 1
    rows = part_ref.shape[2]
    products = []
    for which, out_ref in enumerate((own_ref, core_ref)):
        real = (part_ref[which, 0] + other_ref[1 - which, 0])[:, :count]
        imag = (part_ref[which, 1] + other_ref[1 - which, 1])[:, :count]
        out_ref[count : count + rows, :count] = real
        out_ref[count + rows :, :count] = imag
        both = jnp.concatenate([real, imag], axis=1)
        products.append(exact(both, both, ((0,), (0,))))
    product = products[0] + products[1]
    gram_re = product[:count, :count] + product[count:, count:]
    gram_im = product[:count, count:] - product[count:, :count]
    row = lax.broadcasted_iota(jnp.int32, gram_re.shape, 0)
    column = lax.broadcasted_iota(jnp.int32, gram_re.shape, 1)
    own_ref[:count, :count] = jnp.where(row <= column, gram_re, gram_im)
    peak = part_ref[0, 0, :1, count:] + other_ref[0, 0, :1, count:]
    own_ref[:, count:] = jnp.broadcast_to(peak, (own_ref.shape[0], 1))


def eliminate(real, imag):
    count, width = real.shape
    lane = lax.broadcasted_iota(jnp.int32, (ROWS, width), 1)
    row = lax.broadcasted_iota(jnp.int32, (ROWS, width), 0)
    blocks = count // ROWS
    re = [real[ROWS * i : ROWS * (i + 1)] for i in range(blocks)]
    im = [imag[ROWS * i : ROWS * (i + 1)] for i in range(blocks)]
    out_re, out_im = [], []
    spread = lambda value: jnp.broadcast_to(value, (ROWS, width))
    pick = lambda value, at: spread(value[at : at + 1])
    solved = None
    for b in range(blocks):
        first = ROWS * b
        if b:
            old = first - ROWS
            cleared = (lane >= old) & (lane < first)
            next_re, next_im = jnp.where(cleared, 0.0, re[b]), jnp.where(cleared, 0.0, im[b])
            parts_re, parts_im = [], []
            for o in range(ROWS):
                c_re, c_im = spread(re[b][:, old + o : old + o + 1]), spread(im[b][:, old + o : old + o + 1])
                s_re, s_im = pick(solved[0], o), pick(solved[1], o)
                parts_re.append(c_re * s_re - c_im * s_im)
                parts_im.append(c_re * s_im + c_im * s_re)
            while len(parts_re) > 1:
                parts_re = [left + right for left, right in zip(parts_re[0::2], parts_re[1::2])]
                parts_im = [left + right for left, right in zip(parts_im[0::2], parts_im[1::2])]
            re[b], im[b] = next_re - parts_re[0], next_im - parts_im[0]
            if b + 1 < blocks:
                rest_re, rest_im = jnp.concatenate(re[b + 1 :]), jnp.concatenate(im[b + 1 :])
                columns = jnp.concatenate([rest_re[:, old:first], rest_im[:, old:first]], axis=1)
                weights = jnp.concatenate(
                    [
                        jnp.concatenate([solved[0], solved[1]], axis=1),
                        jnp.concatenate([-solved[1], solved[0]], axis=1),
                    ]
                )
                taken = exact(columns, weights, ((1,), (0,)))
                for at, i in enumerate(range(b + 1, blocks)):
                    some = slice(ROWS * at, ROWS * (at + 1))
                    re[i] = jnp.where(cleared, 0.0, re[i]) - taken[some, :width]
                    im[i] = jnp.where(cleared, 0.0, im[i]) - taken[some, width:]
        x_re, x_im = re[b], im[b]
        done_re, done_im = x_re, x_im
        col_re = [spread(x_re[:, first + o : first + o + 1]) for o in range(ROWS)]
        col_im = [spread(x_im[:, first + o : first + o + 1]) for o in range(ROWS)]
        live_re, live_im = list(col_re), list(col_im)
        for o in range(0, ROWS, 2):
            hit0, hit1 = lane == first + o, lane == first + o + 1
            hit = hit0 | hit1
            row0 = row == o
            pair = row0 | (row == o + 1)
            a, c = pick(live_re[o], o), pick(live_re[o + 1], o + 1)
            f_re, f_im = pick(live_re[o], o + 1), pick(live_im[o], o + 1)
            root = lax.rsqrt(a * c - (f_re * f_re + f_im * f_im))
            inverse = root * root

            def solve(re0, im0, re1, im1):
                return (
                    c * re0 - (f_re * re1 + f_im * im1),
                    c * im0 - (f_re * im1 - f_im * re1),
                    a * re1 - (f_re * re0 - f_im * im0),
                    a * im1 - (f_re * im0 + f_im * re0),
                )

            def less(z0_re, z0_im, z1_re, z1_im):
                return (
                    (col_re[o] * z0_re - col_im[o] * z0_im) + (col_re[o + 1] * z1_re - col_im[o + 1] * z1_im),
                    (col_re[o] * z0_im + col_im[o] * z0_re) + (col_re[o + 1] * z1_im + col_im[o + 1] * z1_re),
                )

            for j in range(o + 2, ROWS):
                z = solve(pick(live_re[j], o), pick(live_im[j], o), pick(live_re[j], o + 1), pick(live_im[j], o + 1))
                off_re, off_im = less(*z)
                live_re[j] = col_re[j] - off_re * inverse
                live_im[j] = col_im[j] - off_im * inverse
                col_re[j] = jnp.where(pair, jnp.where(row0, z[0], z[2]) * inverse, live_re[j])
                col_im[j] = jnp.where(pair, jnp.where(row0, z[1], z[3]) * inverse, live_im[j])
            re0 = jnp.where(hit0, 1.0, jnp.where(hit1, 0.0, pick(x_re, o)))
            re1 = jnp.where(hit1, 1.0, jnp.where(hit0, 0.0, pick(x_re, o + 1)))
            im0, im1 = jnp.where(hit, 0.0, pick(x_im, o)), jnp.where(hit, 0.0, pick(x_im, o + 1))
            z = solve(re0, im0, re1, im1)
            scale0 = lax.rsqrt(a)
            scale1 = root * scale0
            done_re = jnp.where(row0, re0 * scale0, jnp.where(pair, z[2] * scale1, done_re))
            done_im = jnp.where(row0, im0 * scale0, jnp.where(pair, z[3] * scale1, done_im))
            off_re, off_im = less(*z)
            x_re = jnp.where(
                pair, jnp.where(row0, z[0], z[2]) * inverse, jnp.where(hit, 0.0, x_re) - off_re * inverse
            )
            x_im = jnp.where(
                pair, jnp.where(row0, z[1], z[3]) * inverse, jnp.where(hit, 0.0, x_im) - off_im * inverse
            )
        out_re.append(done_re)
        out_im.append(done_im)
        solved = (x_re, x_im)
    return jnp.concatenate(out_re), jnp.concatenate(out_im)


def basis_kernel(scale, *refs):
    sketched, gram_ref, basis_ref, weights = refs[:GROUPS], refs[GROUPS], refs[GROUPS + 1], refs[GROUPS + 2 :]
    count = gram_ref.shape[0]
    rows = basis_ref.shape[1]
    packed = gram_ref[:, :count]
    flipped = packed.T
    row = lax.broadcasted_iota(jnp.int32, packed.shape, 0)
    column = lax.broadcasted_iota(jnp.int32, packed.shape, 1)
    gram_re = jnp.where(row <= column, packed, flipped)
    gram_im = jnp.where(row > column, packed, jnp.where(row < column, -flipped, 0.0))
    diagonal = jnp.where(row == column, gram_re, 0.0)
    across = lax.rsqrt(jnp.sum(diagonal, axis=0, keepdims=True))
    down = lax.rsqrt(jnp.sum(diagonal, axis=1, keepdims=True))
    padding = [(0, 0), (0, -count % 128)]
    low_re, low_im = eliminate(
        jnp.pad(gram_re * down * across, padding), jnp.pad(gram_im * down * across, padding)
    )
    low_re = jnp.where(row >= column, low_re[:, :count] * across, 0.0)
    low_im = jnp.where(row >= column, low_im[:, :count] * across, 0.0)
    stacked = jnp.concatenate([ref[count:, :count] for ref in sketched], axis=0)
    by_re = exact(stacked, low_re, ((1,), (1,)))
    by_im = exact(stacked, low_im, ((1,), (1,)))
    for group in range(GROUPS):
        real = slice(2 * rows * group, 2 * rows * group + rows)
        imag = slice(2 * rows * group + rows, 2 * rows * (group + 1))
        ortho_re = by_re[real] + by_im[imag]
        ortho_im = by_re[imag] - by_im[real]
        if group == 0:
            basis_ref[0] = ortho_re * scale
            basis_ref[1] = ortho_im * scale
        flat_re, flat_im = ortho_re.T, ortho_im.T
        top = jnp.concatenate([flat_re, flat_im], axis=1)
        low = jnp.concatenate([-flat_im, flat_re], axis=1)
        weights[group][...] = jnp.concatenate([top, low], axis=0).astype(jnp.bfloat16)


def folds(rows, share):
    whole = share // 128 * 128
    rest = share - whole
    count = whole // rest if rest else 0
    return count if count and rows % (16 * count) == 0 else 0


def folded_shape(rows, share):
    count = folds(rows, share)
    return (rows + rows // count, share // 128 * 128) if count else (rows, share)


def fold(value):
    rows, share = value.shape
    count = folds(rows, share)
    if not count:
        return value
    whole, each = share // 128 * 128, rows // count
    rest = [value[each * i : each * (i + 1), whole:] for i in range(count)]
    spare = whole - count * (share - whole)
    if spare:
        rest.append(jnp.zeros((each, spare), value.dtype))
    return jnp.concatenate([value[:, :whole], jnp.concatenate(rest, axis=1)], axis=0)


def fold_kernel(sketch_ref, out_ref):
    out_ref[0] = fold(jnp.concatenate([sketch_ref[0], sketch_ref[1]], axis=0))


def unfold(value, rows, share):
    count = folds(rows, share)
    if not count:
        return value
    wide = share - value.shape[1]
    rest = [value[rows:, wide * i : wide * (i + 1)] for i in range(count)]
    return jnp.concatenate([value[:rows], jnp.concatenate(rest, axis=0)], axis=1)


def project_kernel(bound, gram_ref, *refs):
    weights, (stay_ref, near_ref, far_ref, cross_ref) = refs[:GROUPS], refs[GROUPS : GROUPS + 4]
    core, (own_ref, side_ref, *far_outs) = refs[GROUPS + 4 : GROUPS + 4 + 2 * PARTS], refs[GROUPS + 4 + 2 * PARTS :]
    count = gram_ref.shape[0]
    factor = TOP / (gram_ref[:1, count : count + 1] * bound)
    half = near_ref.shape[0]

    def project(*data):
        total = None
        for weight_ref, block in zip(weights, data):
            term = jnp.dot(weight_ref[...], block, preferred_element_type=jnp.float32)
            total = term if total is None else total + term
        return fold(total * factor)

    for zone in range(half):
        far_outs[zone][...] = project(
            stay_ref[half + zone], of_core(core, 0, half + zone), far_ref[zone], cross_ref[zone]
        )
    for zone in range(half):
        side_ref[zone] = project(near_ref[zone], of_core(core, 1, zone))
        own_ref[zone] = project(stay_ref[zone], of_core(core, 0, zone))


def tied(first, second):
    first, second = list(first), list(second)
    both = lax.optimization_barrier(tuple(first + second))
    return list(both[: len(first)]), list(both[len(first) :])


def gather_slots(piece, size, ahead):
    bits = size.bit_length() - 1
    direct = min(bits, 4)
    have = {0: piece}
    for level in range(1, direct):
        if level == 2:
            first = [1 << bit for bit in reversed(range(1, direct))]
            values = lax.optimization_barrier(tuple(have[slot] for slot in first))
            have.update(zip(first, values))
        for slot in range(0, 1 << direct, 2):
            if slot.bit_count() == level:
                along = slot & -slot if slot >> direct - 1 else 1 << slot.bit_length() - 1
                have[slot] = swap(have[slot ^ along], along, size)
    pieces = [(have[slot], [slot]) for slot in sorted(have, key=lambda slot: (slot.bit_count(), slot))]
    for bit in range(4, bits):
        whole = jnp.concatenate([value for value, _ in pieces])
        slots = [slot for _, held in pieces for slot in held]
        pieces = [(whole, slots), (swap(whole, 1 << bit, size), [slot | 1 << bit for slot in slots])]
    return pieces


def per_device(traces, sketch):
    size = lax.axis_size("rcv")
    me = lax.axis_index("rcv")
    rows, sources = traces.shape[1:]
    count, share = sketch.shape[1:]
    zones = size // GROUPS
    half = zones // 2
    bits = size.bit_length() - 1
    chunk = lambda slots: jax.ShapeDtypeStruct((slots, 2 * rows, share), traces.dtype)

    stay, near, far, cross, peak, *core = pl.pallas_call(
        functools.partial(chunk_kernel, share),
        out_shape=(
            chunk(zones),
            chunk(half),
            chunk(half),
            chunk(half),
            jax.ShapeDtypeStruct((1, sources), jnp.float32),
        )
        + (chunk(zones // PARTS),) * (2 * PARTS),
        in_specs=[SMEM, VMEM],
        out_specs=(VMEM,) * (5 + 2 * PARTS),
        scratch_shapes=[pltpu.VMEM((GROUPS, zones, 2 * rows, share), traces.dtype)],
        compiler_params=PARAMS,
        name="source_chunks",
    )(me.astype(jnp.int32).reshape(1), traces)
    core_in = [swap(value, 1, size) for value in core]
    piece = pl.pallas_call(
        fold_kernel,
        out_shape=jax.ShapeDtypeStruct((1, *folded_shape(2 * count, share)), sketch.dtype),
        in_specs=[VMEM],
        out_specs=VMEM,
        compiler_params=PARAMS,
        name="fold_columns",
    )(sketch)
    pieces = gather_slots(piece, size, stay)
    values = [value for value, _ in pieces]
    held = {slot: (which, at) for which, (_, slots) in enumerate(pieces) for at, slot in enumerate(slots)}
    partial = pl.pallas_call(
        functools.partial(sketch_kernel, held),
        out_shape=jax.ShapeDtypeStruct((2, 2, rows, count + 1), jnp.float32),
        in_specs=[VMEM] * (4 + 2 * PARTS + len(values)),
        out_specs=VMEM,
        compiler_params=PARAMS,
        name="sketch_rows",
    )(peak, stay, near, far, *core_in, *values)
    packet = jax.ShapeDtypeStruct((count + 2 * rows, count + 1), jnp.float32)
    own_packet, core_packet = pl.pallas_call(
        gram_kernel,
        out_shape=(packet, packet),
        in_specs=[VMEM] * 2,
        out_specs=(VMEM, VMEM),
        compiler_params=PARAMS,
        name="chip_gram",
    )(partial, swap(partial, 1, size))

    beside = swap(own_packet, 2, size)
    known = [own_packet, core_packet, beside, swap(beside, 1, size)]
    (far_out, cross_out), _ = tied([far, cross], [own_packet])
    far_in, cross_in = swap(far_out, 2, size), swap(cross_out, 3, size)
    gram = own_packet[:count] + beside[:count]
    for bit in range(2, bits):
        gram = gram + swap(gram, 1 << bit, size)

    basis, *weights = pl.pallas_call(
        functools.partial(basis_kernel, math.sqrt(rows * size)),
        out_shape=(jax.ShapeDtypeStruct((2, rows, count), jnp.float32),)
        + (jax.ShapeDtypeStruct((2 * count, 2 * rows), jnp.bfloat16),) * GROUPS,
        in_specs=[VMEM] * (1 + GROUPS),
        out_specs=(VMEM,) * (1 + GROUPS),
        compiler_params=PARAMS,
        cost_estimate=pl.CostEstimate(flops=1_500_000_000, bytes_accessed=1_000_000, transcendentals=0),
        name="orthonormal_basis",
    )(*known, gram)
    folded = folded_shape(2 * count, share)
    bound = 1.01 * math.sqrt(2 * rows * size)
    own, side, *away = pl.pallas_call(
        functools.partial(project_kernel, bound),
        out_shape=(
            jax.ShapeDtypeStruct((half, *folded), jnp.float32),
            jax.ShapeDtypeStruct((half, *folded), jnp.float32),
        )
        + (jax.ShapeDtypeStruct(folded, jnp.float32),) * half,
        in_specs=[VMEM] * (1 + GROUPS + 4 + 2 * PARTS),
        out_specs=(VMEM,) * (2 + half),
        compiler_params=PARAMS,
        name="project_rows",
    )(gram, *weights, stay, near, far_in, cross_in, *core_in)

    send = lambda value, mask: swap(value.astype(jnp.float16), mask, size).astype(jnp.float32)
    if zones <= 4:
        side = send(side, 2)
        parts = [send(away[zone], GROUPS * (half + zone)) for zone in reversed(range(half))]
        parts += [send(own[zone] + side[zone], GROUPS * zone) for zone in range(1, half)]
        total = own[0] + side[0] + sum(parts)
    else:
        total = own + send(side, 2) + send(jnp.stack(away), GROUPS * half)
        while total.shape[0] > 1:
            low, high = jnp.split(total, 2)
            total = low + send(high, GROUPS * low.shape[0])
        total = total[0]
    level = gram[:1, count:] * bound
    total = total * (level / TOP)
    total = unfold(total, 2 * count, share)
    return basis, total.reshape(2, count, share)


def solution(mesh):
    return jax.shard_map(
        per_device,
        mesh=mesh,
        in_specs=(P(None, ("grp", "rcv"), None), P(None, None, "rcv")),
        out_specs=(P(None, ("grp", "rcv"), None), P(None, "grp", "rcv")),
        check_vma=False,
    )
```

```python
import functools
import math

import jax
import jax.numpy as jnp
from jax import lax
from jax.experimental import pallas as pl
from jax.experimental.pallas import tpu as pltpu
from jax.sharding import PartitionSpec as P

ROWS = 8
GROUPS = 4
PARTS = 2
TOP = 32768.0
VMEM = pl.BlockSpec(memory_space=pltpu.VMEM)
SMEM = pl.BlockSpec(memory_space=pltpu.SMEM)
PARAMS = pltpu.CompilerParams(vmem_limit_bytes=40 * 1024 * 1024)


def swap(value, mask, size):
    return lax.ppermute(value, "rcv", [(i, i ^ mask) for i in range(size)])


def exact(left, right, dims):
    return lax.dot_general(
        left,
        right,
        ((dims[0], dims[1]), ((), ())),
        precision=lax.Precision.HIGHEST,
        preferred_element_type=jnp.float32,
    )


def chunk_kernel(share, me_ref, traces_ref, stay_ref, near_ref, far_ref, cross_ref, *refs):
    core, held_ref = refs[:-1], refs[-1]
    rows, sources = traces_ref.shape[1:]
    me = me_ref[0]
    for owner in range(sources // share):
        away = owner ^ me
        for part in range(2):
            held_ref[away % GROUPS, away // GROUPS, rows * part : rows * (part + 1), :] = traces_ref[
                part, :, owner * share : (owner + 1) * share
            ]
    zones, half = stay_ref.shape[0], near_ref.shape[0]
    for at, ref in enumerate(core):
        first = at % PARTS * ref.shape[0]
        ref[...] = held_ref[1 + at // PARTS * 2, first : first + ref.shape[0]]
    stay_ref[...] = held_ref[0]
    near_ref[...] = held_ref[2, :half]
    far_ref[...] = held_ref[2, half:]
    cross_ref[...] = held_ref[3, half:]


def peak_kernel(*refs):
    peak = None
    for ref in refs[:-1]:
        for zone in range(ref.shape[0]):
            largest = jnp.max(jnp.abs(ref[zone]), axis=0, keepdims=True)
            peak = largest if peak is None else jnp.maximum(peak, largest)
    refs[-1][...] = peak.astype(jnp.float32)


def of_core(core, beside, zone):
    each = core[0].shape[0]
    return core[beside * PARTS + zone // each][zone % each]


def sketch_kernel(held, peak_ref, stay_ref, near_ref, far_ref, *refs):
    core, pieces, out_ref = refs[: 2 * PARTS], refs[2 * PARTS : -1], refs[-1]
    count = out_ref.shape[-1] - 1
    zones, half = stay_ref.shape[0], near_ref.shape[0]
    totals = [None, None]
    for slot in range(0, GROUPS * zones, 2):
        beside, zone = slot % GROUPS // 2, slot // GROUPS
        if beside:
            own = near_ref[zone] if zone < half else far_ref[zone - half]
        else:
            own = stay_ref[zone]
        which, at = held[slot]
        block = unfold(pieces[which][at], 2 * count, own.shape[1])
        for rows, data in enumerate((own, of_core(core, beside, zone))):
            term = lax.dot_general(data, block, (((1,), (1,)), ((), ())), preferred_element_type=jnp.float32)
            totals[rows] = term if totals[rows] is None else totals[rows] + term
    for part, total in enumerate(totals):
        rows = total.shape[0] // 2
        out_ref[part, 0, :, :count] = total[:rows, :count] - total[rows:, count:]
        out_ref[part, 1, :, :count] = total[:rows, count:] + total[rows:, :count]
    peak = jnp.max(peak_ref[...], axis=1, keepdims=True)
    out_ref[:, :, :, count:] = jnp.broadcast_to(peak[None, None], out_ref.shape[:3] + (1,))


def gram_kernel(part_ref, other_ref, own_ref, core_ref):
    count = part_ref.shape[-1] - 1
    rows = part_ref.shape[2]
    products = []
    for which, out_ref in enumerate((own_ref, core_ref)):
        real = (part_ref[which, 0] + other_ref[1 - which, 0])[:, :count]
        imag = (part_ref[which, 1] + other_ref[1 - which, 1])[:, :count]
        out_ref[count : count + rows, :count] = real
        out_ref[count + rows :, :count] = imag
        both = jnp.concatenate([real, imag], axis=1)
        products.append(exact(both, both, ((0,), (0,))))
    product = products[0] + products[1]
    gram_re = product[:count, :count] + product[count:, count:]
    gram_im = product[:count, count:] - product[count:, :count]
    row = lax.broadcasted_iota(jnp.int32, gram_re.shape, 0)
    column = lax.broadcasted_iota(jnp.int32, gram_re.shape, 1)
    own_ref[:count, :count] = jnp.where(row <= column, gram_re, gram_im)
    peak = part_ref[0, 0, :1, count:] + other_ref[0, 0, :1, count:]
    own_ref[:, count:] = jnp.broadcast_to(peak, (own_ref.shape[0], 1))


def eliminate(real, imag):
    count, width = real.shape
    lane = lax.broadcasted_iota(jnp.int32, (ROWS, width), 1)
    row = lax.broadcasted_iota(jnp.int32, (ROWS, width), 0)
    blocks = count // ROWS
    re = [real[ROWS * i : ROWS * (i + 1)] for i in range(blocks)]
    im = [imag[ROWS * i : ROWS * (i + 1)] for i in range(blocks)]
    out_re, out_im = [], []
    spread = lambda value: jnp.broadcast_to(value, (ROWS, width))
    pick = lambda value, at: spread(value[at : at + 1])
    solved = None
    for b in range(blocks):
        first = ROWS * b
        if b:
            old = first - ROWS
            cleared = (lane >= old) & (lane < first)
            next_re, next_im = jnp.where(cleared, 0.0, re[b]), jnp.where(cleared, 0.0, im[b])
            parts_re, parts_im = [], []
            for o in range(ROWS):
                c_re, c_im = spread(re[b][:, old + o : old + o + 1]), spread(im[b][:, old + o : old + o + 1])
                s_re, s_im = pick(solved[0], o), pick(solved[1], o)
                parts_re.append(c_re * s_re - c_im * s_im)
                parts_im.append(c_re * s_im + c_im * s_re)
            while len(parts_re) > 1:
                parts_re = [left + right for left, right in zip(parts_re[0::2], parts_re[1::2])]
                parts_im = [left + right for left, right in zip(parts_im[0::2], parts_im[1::2])]
            re[b], im[b] = next_re - parts_re[0], next_im - parts_im[0]
            if b + 1 < blocks:
                rest_re, rest_im = jnp.concatenate(re[b + 1 :]), jnp.concatenate(im[b + 1 :])
                columns = jnp.concatenate([rest_re[:, old:first], rest_im[:, old:first]], axis=1)
                weights = jnp.concatenate(
                    [
                        jnp.concatenate([solved[0], solved[1]], axis=1),
                        jnp.concatenate([-solved[1], solved[0]], axis=1),
                    ]
                )
                taken = exact(columns, weights, ((1,), (0,)))
                for at, i in enumerate(range(b + 1, blocks)):
                    some = slice(ROWS * at, ROWS * (at + 1))
                    re[i] = jnp.where(cleared, 0.0, re[i]) - taken[some, :width]
                    im[i] = jnp.where(cleared, 0.0, im[i]) - taken[some, width:]
        x_re, x_im = re[b], im[b]
        done_re, done_im = x_re, x_im
        col_re = [spread(x_re[:, first + o : first + o + 1]) for o in range(ROWS)]
        col_im = [spread(x_im[:, first + o : first + o + 1]) for o in range(ROWS)]
        live_re, live_im = list(col_re), list(col_im)
        for o in range(0, ROWS, 2):
            hit0, hit1 = lane == first + o, lane == first + o + 1
            hit = hit0 | hit1
            row0 = row == o
            pair = row0 | (row == o + 1)
            a, c = pick(live_re[o], o), pick(live_re[o + 1], o + 1)
            f_re, f_im = pick(live_re[o], o + 1), pick(live_im[o], o + 1)
            root = lax.rsqrt(a * c - (f_re * f_re + f_im * f_im))
            inverse = root * root

            def solve(re0, im0, re1, im1):
                return (
                    c * re0 - (f_re * re1 + f_im * im1),
                    c * im0 - (f_re * im1 - f_im * re1),
                    a * re1 - (f_re * re0 - f_im * im0),
                    a * im1 - (f_re * im0 + f_im * re0),
                )

            def less(z0_re, z0_im, z1_re, z1_im):
                return (
                    (col_re[o] * z0_re - col_im[o] * z0_im) + (col_re[o + 1] * z1_re - col_im[o + 1] * z1_im),
                    (col_re[o] * z0_im + col_im[o] * z0_re) + (col_re[o + 1] * z1_im + col_im[o + 1] * z1_re),
                )

            for j in range(o + 2, ROWS):
                z = solve(pick(live_re[j], o), pick(live_im[j], o), pick(live_re[j], o + 1), pick(live_im[j], o + 1))
                off_re, off_im = less(*z)
                live_re[j] = col_re[j] - off_re * inverse
                live_im[j] = col_im[j] - off_im * inverse
                col_re[j] = jnp.where(pair, jnp.where(row0, z[0], z[2]) * inverse, live_re[j])
                col_im[j] = jnp.where(pair, jnp.where(row0, z[1], z[3]) * inverse, live_im[j])
            re0 = jnp.where(hit0, 1.0, jnp.where(hit1, 0.0, pick(x_re, o)))
            re1 = jnp.where(hit1, 1.0, jnp.where(hit0, 0.0, pick(x_re, o + 1)))
            im0, im1 = jnp.where(hit, 0.0, pick(x_im, o)), jnp.where(hit, 0.0, pick(x_im, o + 1))
            z = solve(re0, im0, re1, im1)
            scale0 = lax.rsqrt(a)
            scale1 = root * scale0
            done_re = jnp.where(row0, re0 * scale0, jnp.where(pair, z[2] * scale1, done_re))
            done_im = jnp.where(row0, im0 * scale0, jnp.where(pair, z[3] * scale1, done_im))
            off_re, off_im = less(*z)
            x_re = jnp.where(
                pair, jnp.where(row0, z[0], z[2]) * inverse, jnp.where(hit, 0.0, x_re) - off_re * inverse
            )
            x_im = jnp.where(
                pair, jnp.where(row0, z[1], z[3]) * inverse, jnp.where(hit, 0.0, x_im) - off_im * inverse
            )
        out_re.append(done_re)
        out_im.append(done_im)
        solved = (x_re, x_im)
    return jnp.concatenate(out_re), jnp.concatenate(out_im)


def basis_kernel(scale, *refs):
    sketched, gram_ref, basis_ref, weights = refs[:GROUPS], refs[GROUPS], refs[GROUPS + 1], refs[GROUPS + 2 :]
    count = gram_ref.shape[0]
    rows = basis_ref.shape[1]
    packed = gram_ref[:, :count]
    flipped = packed.T
    row = lax.broadcasted_iota(jnp.int32, packed.shape, 0)
    column = lax.broadcasted_iota(jnp.int32, packed.shape, 1)
    gram_re = jnp.where(row <= column, packed, flipped)
    gram_im = jnp.where(row > column, packed, jnp.where(row < column, -flipped, 0.0))
    diagonal = jnp.where(row == column, gram_re, 0.0)
    across = lax.rsqrt(jnp.sum(diagonal, axis=0, keepdims=True))
    down = lax.rsqrt(jnp.sum(diagonal, axis=1, keepdims=True))
    padding = [(0, 0), (0, -count % 128)]
    low_re, low_im = eliminate(
        jnp.pad(gram_re * down * across, padding), jnp.pad(gram_im * down * across, padding)
    )
    low_re = jnp.where(row >= column, low_re[:, :count] * across, 0.0)
    low_im = jnp.where(row >= column, low_im[:, :count] * across, 0.0)
    stacked = jnp.concatenate([ref[count:, :count] for ref in sketched], axis=0)
    spare = jnp.zeros((-count % 128, count), jnp.float32)
    both = exact(stacked, jnp.concatenate([low_re, spare, low_im], axis=0), ((1,), (1,)))
    by_re, by_im = both[:, :count], both[:, count + spare.shape[0] :]
    for group in range(GROUPS):
        real = slice(2 * rows * group, 2 * rows * group + rows)
        imag = slice(2 * rows * group + rows, 2 * rows * (group + 1))
        ortho_re = by_re[real] + by_im[imag]
        ortho_im = by_re[imag] - by_im[real]
        if group == 0:
            basis_ref[0] = ortho_re * scale
            basis_ref[1] = ortho_im * scale
        flat_re, flat_im = ortho_re.T, ortho_im.T
        top = jnp.concatenate([flat_re, flat_im], axis=1)
        low = jnp.concatenate([-flat_im, flat_re], axis=1)
        weights[group][...] = jnp.concatenate([top, low], axis=0).astype(jnp.bfloat16)


def folds(rows, share):
    whole = share // 128 * 128
    rest = share - whole
    count = whole // rest if rest else 0
    return count if count and rows % (16 * count) == 0 else 0


def folded_shape(rows, share):
    count = folds(rows, share)
    return (rows + rows // count, share // 128 * 128) if count else (rows, share)


def fold(value):
    rows, share = value.shape
    count = folds(rows, share)
    if not count:
        return value
    whole, each = share // 128 * 128, rows // count
    rest = [value[each * i : each * (i + 1), whole:] for i in range(count)]
    spare = whole - count * (share - whole)
    if spare:
        rest.append(jnp.zeros((each, spare), value.dtype))
    return jnp.concatenate([value[:, :whole], jnp.concatenate(rest, axis=1)], axis=0)


def fold_kernel(sketch_ref, out_ref):
    out_ref[0] = fold(jnp.concatenate([sketch_ref[0], sketch_ref[1]], axis=0))


def unfold(value, rows, share):
    count = folds(rows, share)
    if not count:
        return value
    wide = share - value.shape[1]
    rest = [value[rows:, wide * i : wide * (i + 1)] for i in range(count)]
    return jnp.concatenate([value[:rows], jnp.concatenate(rest, axis=0)], axis=1)


def project_kernel(bound, gram_ref, *refs):
    weights, (stay_ref, near_ref, far_ref, cross_ref) = refs[:GROUPS], refs[GROUPS : GROUPS + 4]
    core, (own_ref, side_ref, *far_outs) = refs[GROUPS + 4 : GROUPS + 4 + 2 * PARTS], refs[GROUPS + 4 + 2 * PARTS :]
    count = gram_ref.shape[0]
    factor = TOP / (gram_ref[:1, count : count + 1] * bound)
    half = near_ref.shape[0]

    def project(*data):
        total = None
        for weight_ref, block in zip(weights, data):
            term = jnp.dot(weight_ref[...], block, preferred_element_type=jnp.float32)
            total = term if total is None else total + term
        return fold(total * factor)

    for zone in range(half):
        far_outs[zone][...] = project(
            stay_ref[half + zone], of_core(core, 0, half + zone), far_ref[zone], cross_ref[zone]
        )
    for zone in range(half):
        side_ref[zone] = project(near_ref[zone], of_core(core, 1, zone))
        own_ref[zone] = project(stay_ref[zone], of_core(core, 0, zone))


def tied(first, second):
    first, second = list(first), list(second)
    both = lax.optimization_barrier(tuple(first + second))
    return list(both[: len(first)]), list(both[len(first) :])


def gather_slots(piece, size, ahead):
    bits = size.bit_length() - 1
    direct = min(bits, 4)
    have = {0: piece}
    for level in range(1, direct):
        if level == 2:
            first = [1 << bit for bit in reversed(range(1, direct))]
            values = lax.optimization_barrier(tuple(have[slot] for slot in first))
            have.update(zip(first, values))
        for slot in range(0, 1 << direct, 2):
            if slot.bit_count() == level:
                along = slot & -slot if slot >> direct - 1 else 1 << slot.bit_length() - 1
                have[slot] = swap(have[slot ^ along], along, size)
    pieces = [(have[slot], [slot]) for slot in sorted(have, key=lambda slot: (slot.bit_count(), slot))]
    for bit in range(4, bits):
        whole = jnp.concatenate([value for value, _ in pieces])
        slots = [slot for _, held in pieces for slot in held]
        pieces = [(whole, slots), (swap(whole, 1 << bit, size), [slot | 1 << bit for slot in slots])]
    return pieces


def per_device(traces, sketch):
    size = lax.axis_size("rcv")
    me = lax.axis_index("rcv")
    rows, sources = traces.shape[1:]
    count, share = sketch.shape[1:]
    zones = size // GROUPS
    half = zones // 2
    bits = size.bit_length() - 1
    chunk = lambda slots: jax.ShapeDtypeStruct((slots, 2 * rows, share), traces.dtype)

    stay, near, far, cross, *core = pl.pallas_call(
        functools.partial(chunk_kernel, share),
        out_shape=(
            chunk(zones),
            chunk(half),
            chunk(half),
            chunk(half),
        )
        + (chunk(zones // PARTS),) * (2 * PARTS),
        in_specs=[SMEM, VMEM],
        out_specs=(VMEM,) * (4 + 2 * PARTS),
        scratch_shapes=[pltpu.VMEM((GROUPS, zones, 2 * rows, share), traces.dtype)],
        compiler_params=PARAMS,
        name="source_chunks",
    )(me.astype(jnp.int32).reshape(1), traces)
    core_in = [swap(value, 1, size) for value in core]
    peak = pl.pallas_call(
        peak_kernel,
        out_shape=jax.ShapeDtypeStruct((1, share), jnp.float32),
        in_specs=[VMEM] * (4 + 2 * PARTS),
        out_specs=VMEM,
        compiler_params=PARAMS,
        name="largest_value",
    )(stay, near, far, cross, *core)
    piece = pl.pallas_call(
        fold_kernel,
        out_shape=jax.ShapeDtypeStruct((1, *folded_shape(2 * count, share)), sketch.dtype),
        in_specs=[VMEM],
        out_specs=VMEM,
        compiler_params=PARAMS,
        name="fold_columns",
    )(sketch)
    pieces = gather_slots(piece, size, stay)
    values = [value for value, _ in pieces]
    held = {slot: (which, at) for which, (_, slots) in enumerate(pieces) for at, slot in enumerate(slots)}
    partial = pl.pallas_call(
        functools.partial(sketch_kernel, held),
        out_shape=jax.ShapeDtypeStruct((2, 2, rows, count + 1), jnp.float32),
        in_specs=[VMEM] * (4 + 2 * PARTS + len(values)),
        out_specs=VMEM,
        compiler_params=PARAMS,
        name="sketch_rows",
    )(peak, stay, near, far, *core_in, *values)
    packet = jax.ShapeDtypeStruct((count + 2 * rows, count + 1), jnp.float32)
    own_packet, core_packet = pl.pallas_call(
        gram_kernel,
        out_shape=(packet, packet),
        in_specs=[VMEM] * 2,
        out_specs=(VMEM, VMEM),
        compiler_params=PARAMS,
        name="chip_gram",
    )(partial, swap(partial, 1, size))

    beside = swap(own_packet, 2, size)
    known = [own_packet, core_packet, beside, swap(beside, 1, size)]
    (far_out, cross_out), _ = tied([far, cross], [own_packet])
    far_in, cross_in = swap(far_out, 2, size), swap(cross_out, 3, size)
    gram = own_packet[:count] + beside[:count]
    for bit in range(2, bits):
        gram = gram + swap(gram, 1 << bit, size)

    basis, *weights = pl.pallas_call(
        functools.partial(basis_kernel, math.sqrt(rows * size)),
        out_shape=(jax.ShapeDtypeStruct((2, rows, count), jnp.float32),)
        + (jax.ShapeDtypeStruct((2 * count, 2 * rows), jnp.bfloat16),) * GROUPS,
        in_specs=[VMEM] * (1 + GROUPS),
        out_specs=(VMEM,) * (1 + GROUPS),
        compiler_params=PARAMS,
        cost_estimate=pl.CostEstimate(flops=1_500_000_000, bytes_accessed=1_000_000, transcendentals=0),
        name="orthonormal_basis",
    )(*known, gram)
    folded = folded_shape(2 * count, share)
    bound = 1.01 * math.sqrt(2 * rows * size)
    own, side, *away = pl.pallas_call(
        functools.partial(project_kernel, bound),
        out_shape=(
            jax.ShapeDtypeStruct((half, *folded), jnp.float32),
            jax.ShapeDtypeStruct((half, *folded), jnp.float32),
        )
        + (jax.ShapeDtypeStruct(folded, jnp.float32),) * half,
        in_specs=[VMEM] * (1 + GROUPS + 4 + 2 * PARTS),
        out_specs=(VMEM,) * (2 + half),
        compiler_params=PARAMS,
        name="project_rows",
    )(gram, *weights, stay, near, far_in, cross_in, *core_in)

    send = lambda value, mask: swap(value.astype(jnp.float16), mask, size).astype(jnp.float32)
    if zones <= 4:
        side = send(side, 2)
        parts = [send(away[zone], GROUPS * (half + zone)) for zone in reversed(range(half))]
        parts += [send(own[zone] + side[zone], GROUPS * zone) for zone in range(1, half)]
        total = own[0] + side[0] + sum(parts)
    else:
        total = own + send(side, 2) + send(jnp.stack(away), GROUPS * half)
        while total.shape[0] > 1:
            low, high = jnp.split(total, 2)
            total = low + send(high, GROUPS * low.shape[0])
        total = total[0]
    level = gram[:1, count:] * bound
    total = total * (level / TOP)
    total = unfold(total, 2 * count, share)
    return basis, total.reshape(2, count, share)


def solution(mesh):
    return jax.shard_map(
        per_device,
        mesh=mesh,
        in_specs=(P(None, ("grp", "rcv"), None), P(None, None, "rcv")),
        out_specs=(P(None, ("grp", "rcv"), None), P(None, "grp", "rcv")),
        check_vma=False,
    )
```

```python
import functools
import math

import jax
import jax.numpy as jnp
from jax import lax
from jax.experimental import pallas as pl
from jax.experimental.pallas import tpu as pltpu
from jax.sharding import PartitionSpec as P

ROWS = 8
GROUPS = 4
PARTS = 2
TOP = 32768.0
VMEM = pl.BlockSpec(memory_space=pltpu.VMEM)
SMEM = pl.BlockSpec(memory_space=pltpu.SMEM)
PARAMS = pltpu.CompilerParams(vmem_limit_bytes=40 * 1024 * 1024)


def swap(value, mask, size):
    return lax.ppermute(value, "rcv", [(i, i ^ mask) for i in range(size)])


def exact(left, right, dims):
    return lax.dot_general(
        left,
        right,
        ((dims[0], dims[1]), ((), ())),
        precision=lax.Precision.HIGHEST,
        preferred_element_type=jnp.float32,
    )


def chunk_kernel(share, me_ref, traces_ref, stay_ref, near_ref, far_ref, cross_ref, peak_ref, *refs):
    core, held_ref = refs[:-1], refs[-1]
    rows, sources = traces_ref.shape[1:]
    me = me_ref[0]
    for owner in range(sources // share):
        away = owner ^ me
        for part in range(2):
            held_ref[away % GROUPS, away // GROUPS, rows * part : rows * (part + 1), :] = traces_ref[
                part, :, owner * share : (owner + 1) * share
            ]
    zones, half = stay_ref.shape[0], near_ref.shape[0]
    for at, ref in enumerate(core):
        first = at % PARTS * ref.shape[0]
        ref[...] = held_ref[1 + at // PARTS * 2, first : first + ref.shape[0]]
    stay_ref[...] = held_ref[0]
    near_ref[...] = held_ref[2, :half]
    far_ref[...] = held_ref[2, half:]
    cross_ref[...] = held_ref[3, half:]
    peak = jnp.maximum(
        jnp.max(jnp.abs(traces_ref[0]), axis=0, keepdims=True),
        jnp.max(jnp.abs(traces_ref[1]), axis=0, keepdims=True),
    )
    peak_ref[...] = peak.astype(jnp.float32)


def of_core(core, beside, zone):
    each = core[0].shape[0]
    return core[beside * PARTS + zone // each][zone % each]


def sketch_kernel(held, peak_ref, stay_ref, near_ref, far_ref, *refs):
    core, pieces, out_ref = refs[: 2 * PARTS], refs[2 * PARTS : -1], refs[-1]
    count = out_ref.shape[-1] - 1
    zones, half = stay_ref.shape[0], near_ref.shape[0]
    totals = [None, None]
    for slot in range(0, GROUPS * zones, 2):
        beside, zone = slot % GROUPS // 2, slot // GROUPS
        if beside:
            own = near_ref[zone] if zone < half else far_ref[zone - half]
        else:
            own = stay_ref[zone]
        which, at = held[slot]
        block = unfold(pieces[which][at], 2 * count, own.shape[1])
        for rows, data in enumerate((own, of_core(core, beside, zone))):
            term = lax.dot_general(data, block, (((1,), (1,)), ((), ())), preferred_element_type=jnp.float32)
            totals[rows] = term if totals[rows] is None else totals[rows] + term
    for part, total in enumerate(totals):
        rows = total.shape[0] // 2
        out_ref[part, 0, :, :count] = total[:rows, :count] - total[rows:, count:]
        out_ref[part, 1, :, :count] = total[:rows, count:] + total[rows:, :count]
    peak = jnp.max(peak_ref[...], axis=1, keepdims=True)
    out_ref[:, :, :, count:] = jnp.broadcast_to(peak[None, None], out_ref.shape[:3] + (1,))


def gram_kernel(part_ref, other_ref, own_ref, core_ref):
    count = part_ref.shape[-1] - 1
    rows = part_ref.shape[2]
    products = []
    for which, out_ref in enumerate((own_ref, core_ref)):
        real = (part_ref[which, 0] + other_ref[1 - which, 0])[:, :count]
        imag = (part_ref[which, 1] + other_ref[1 - which, 1])[:, :count]
        out_ref[count : count + rows, :count] = real
        out_ref[count + rows :, :count] = imag
        both = jnp.concatenate([real, imag], axis=1)
        products.append(exact(both, both, ((0,), (0,))))
    product = products[0] + products[1]
    gram_re = product[:count, :count] + product[count:, count:]
    gram_im = product[:count, count:] - product[count:, :count]
    row = lax.broadcasted_iota(jnp.int32, gram_re.shape, 0)
    column = lax.broadcasted_iota(jnp.int32, gram_re.shape, 1)
    own_ref[:count, :count] = jnp.where(row <= column, gram_re, gram_im)
    peak = part_ref[0, 0, :1, count:] + other_ref[0, 0, :1, count:]
    own_ref[:, count:] = jnp.broadcast_to(peak, (own_ref.shape[0], 1))


def eliminate(real, imag):
    count, width = real.shape
    lane = lax.broadcasted_iota(jnp.int32, (ROWS, width), 1)
    row = lax.broadcasted_iota(jnp.int32, (ROWS, width), 0)
    blocks = count // ROWS
    re = [real[ROWS * i : ROWS * (i + 1)] for i in range(blocks)]
    im = [imag[ROWS * i : ROWS * (i + 1)] for i in range(blocks)]
    out_re, out_im = [], []
    spread = lambda value: jnp.broadcast_to(value, (ROWS, width))
    pick = lambda value, at: spread(value[at : at + 1])
    solved = None
    for b in range(blocks):
        first = ROWS * b
        if b:
            old = first - ROWS
            cleared = (lane >= old) & (lane < first)
            next_re, next_im = jnp.where(cleared, 0.0, re[b]), jnp.where(cleared, 0.0, im[b])
            parts_re, parts_im = [], []
            for o in range(ROWS):
                c_re, c_im = spread(re[b][:, old + o : old + o + 1]), spread(im[b][:, old + o : old + o + 1])
                s_re, s_im = pick(solved[0], o), pick(solved[1], o)
                parts_re.append(c_re * s_re - c_im * s_im)
                parts_im.append(c_re * s_im + c_im * s_re)
            while len(parts_re) > 1:
                parts_re = [left + right for left, right in zip(parts_re[0::2], parts_re[1::2])]
                parts_im = [left + right for left, right in zip(parts_im[0::2], parts_im[1::2])]
            re[b], im[b] = next_re - parts_re[0], next_im - parts_im[0]
            if b + 1 < blocks:
                rest_re, rest_im = jnp.concatenate(re[b + 1 :]), jnp.concatenate(im[b + 1 :])
                columns = jnp.concatenate([rest_re[:, old:first], rest_im[:, old:first]], axis=1)
                weights = jnp.concatenate(
                    [
                        jnp.concatenate([solved[0], solved[1]], axis=1),
                        jnp.concatenate([-solved[1], solved[0]], axis=1),
                    ]
                )
                taken = exact(columns, weights, ((1,), (0,)))
                for at, i in enumerate(range(b + 1, blocks)):
                    some = slice(ROWS * at, ROWS * (at + 1))
                    re[i] = jnp.where(cleared, 0.0, re[i]) - taken[some, :width]
                    im[i] = jnp.where(cleared, 0.0, im[i]) - taken[some, width:]
        x_re, x_im = re[b], im[b]
        done_re, done_im = x_re, x_im
        col_re = [spread(x_re[:, first + o : first + o + 1]) for o in range(ROWS)]
        col_im = [spread(x_im[:, first + o : first + o + 1]) for o in range(ROWS)]
        live_re, live_im = list(col_re), list(col_im)
        for o in range(0, ROWS, 2):
            hit0, hit1 = lane == first + o, lane == first + o + 1
            hit = hit0 | hit1
            row0 = row == o
            pair = row0 | (row == o + 1)
            a, c = pick(live_re[o], o), pick(live_re[o + 1], o + 1)
            f_re, f_im = pick(live_re[o], o + 1), pick(live_im[o], o + 1)
            root = lax.rsqrt(a * c - (f_re * f_re + f_im * f_im))
            inverse = root * root

            def solve(re0, im0, re1, im1):
                return (
                    c * re0 - (f_re * re1 + f_im * im1),
                    c * im0 - (f_re * im1 - f_im * re1),
                    a * re1 - (f_re * re0 - f_im * im0),
                    a * im1 - (f_re * im0 + f_im * re0),
                )

            def less(z0_re, z0_im, z1_re, z1_im):
                return (
                    (col_re[o] * z0_re - col_im[o] * z0_im) + (col_re[o + 1] * z1_re - col_im[o + 1] * z1_im),
                    (col_re[o] * z0_im + col_im[o] * z0_re) + (col_re[o + 1] * z1_im + col_im[o + 1] * z1_re),
                )

            for j in range(o + 2, ROWS):
                z = solve(pick(live_re[j], o), pick(live_im[j], o), pick(live_re[j], o + 1), pick(live_im[j], o + 1))
                off_re, off_im = less(*z)
                live_re[j] = col_re[j] - off_re * inverse
                live_im[j] = col_im[j] - off_im * inverse
                col_re[j] = jnp.where(pair, jnp.where(row0, z[0], z[2]) * inverse, live_re[j])
                col_im[j] = jnp.where(pair, jnp.where(row0, z[1], z[3]) * inverse, live_im[j])
            re0 = jnp.where(hit0, 1.0, jnp.where(hit1, 0.0, pick(x_re, o)))
            re1 = jnp.where(hit1, 1.0, jnp.where(hit0, 0.0, pick(x_re, o + 1)))
            im0, im1 = jnp.where(hit, 0.0, pick(x_im, o)), jnp.where(hit, 0.0, pick(x_im, o + 1))
            z = solve(re0, im0, re1, im1)
            scale0 = lax.rsqrt(a)
            scale1 = root * scale0
            done_re = jnp.where(row0, re0 * scale0, jnp.where(pair, z[2] * scale1, done_re))
            done_im = jnp.where(row0, im0 * scale0, jnp.where(pair, z[3] * scale1, done_im))
            off_re, off_im = less(*z)
            x_re = jnp.where(
                pair, jnp.where(row0, z[0], z[2]) * inverse, jnp.where(hit, 0.0, x_re) - off_re * inverse
            )
            x_im = jnp.where(
                pair, jnp.where(row0, z[1], z[3]) * inverse, jnp.where(hit, 0.0, x_im) - off_im * inverse
            )
        out_re.append(done_re)
        out_im.append(done_im)
        solved = (x_re, x_im)
    return jnp.concatenate(out_re), jnp.concatenate(out_im)


def basis_kernel(scale, *refs):
    sketched, gram_ref, basis_ref, weights = refs[:GROUPS], refs[GROUPS], refs[GROUPS + 1], refs[GROUPS + 2 :]
    count = gram_ref.shape[0]
    rows = basis_ref.shape[1]
    packed = gram_ref[:, :count]
    flipped = packed.T
    row = lax.broadcasted_iota(jnp.int32, packed.shape, 0)
    column = lax.broadcasted_iota(jnp.int32, packed.shape, 1)
    gram_re = jnp.where(row <= column, packed, flipped)
    gram_im = jnp.where(row > column, packed, jnp.where(row < column, -flipped, 0.0))
    diagonal = jnp.where(row == column, gram_re, 0.0)
    across = lax.rsqrt(jnp.sum(diagonal, axis=0, keepdims=True))
    down = lax.rsqrt(jnp.sum(diagonal, axis=1, keepdims=True))
    padding = [(0, 0), (0, -count % 128)]
    low_re, low_im = eliminate(
        jnp.pad(gram_re * down * across, padding), jnp.pad(gram_im * down * across, padding)
    )
    low_re = jnp.where(row >= column, low_re[:, :count] * across, 0.0)
    low_im = jnp.where(row >= column, low_im[:, :count] * across, 0.0)
    stacked = jnp.concatenate([ref[count:, :count] for ref in sketched], axis=0)
    spare = jnp.zeros((-count % 128, count), jnp.float32)
    both = exact(stacked, jnp.concatenate([low_re, spare, low_im], axis=0), ((1,), (1,)))
    by_re, by_im = both[:, :count], both[:, count + spare.shape[0] :]
    for group in range(GROUPS):
        real = slice(2 * rows * group, 2 * rows * group + rows)
        imag = slice(2 * rows * group + rows, 2 * rows * (group + 1))
        ortho_re = by_re[real] + by_im[imag]
        ortho_im = by_re[imag] - by_im[real]
        if group == 0:
            basis_ref[0] = ortho_re * scale
            basis_ref[1] = ortho_im * scale
        flat_re, flat_im = ortho_re.T, ortho_im.T
        top = jnp.concatenate([flat_re, flat_im], axis=1)
        low = jnp.concatenate([-flat_im, flat_re], axis=1)
        weights[group][...] = jnp.concatenate([top, low], axis=0).astype(jnp.bfloat16)


def folds(rows, share):
    whole = share // 128 * 128
    rest = share - whole
    count = whole // rest if rest else 0
    return count if count and rows % (16 * count) == 0 else 0


def folded_shape(rows, share):
    count = folds(rows, share)
    return (rows + rows // count, share // 128 * 128) if count else (rows, share)


def fold(value):
    rows, share = value.shape
    count = folds(rows, share)
    if not count:
        return value
    whole, each = share // 128 * 128, rows // count
    rest = [value[each * i : each * (i + 1), whole:] for i in range(count)]
    spare = whole - count * (share - whole)
    if spare:
        rest.append(jnp.zeros((each, spare), value.dtype))
    return jnp.concatenate([value[:, :whole], jnp.concatenate(rest, axis=1)], axis=0)


def fold_kernel(sketch_ref, out_ref):
    out_ref[0] = fold(jnp.concatenate([sketch_ref[0], sketch_ref[1]], axis=0))


def unfold(value, rows, share):
    count = folds(rows, share)
    if not count:
        return value
    wide = share - value.shape[1]
    rest = [value[rows:, wide * i : wide * (i + 1)] for i in range(count)]
    return jnp.concatenate([value[:rows], jnp.concatenate(rest, axis=0)], axis=1)


def project_kernel(bound, gram_ref, *refs):
    weights, (stay_ref, near_ref, far_ref, cross_ref) = refs[:GROUPS], refs[GROUPS : GROUPS + 4]
    core, (own_ref, side_ref, *far_outs) = refs[GROUPS + 4 : GROUPS + 4 + 2 * PARTS], refs[GROUPS + 4 + 2 * PARTS :]
    count = gram_ref.shape[0]
    factor = TOP / (gram_ref[:1, count : count + 1] * bound)
    half = near_ref.shape[0]

    def project(*data):
        total = None
        for weight_ref, block in zip(weights, data):
            term = jnp.dot(weight_ref[...], block, preferred_element_type=jnp.float32)
            total = term if total is None else total + term
        return fold(total * factor)

    for zone in range(half):
        far_outs[zone][...] = project(
            stay_ref[half + zone], of_core(core, 0, half + zone), far_ref[zone], cross_ref[zone]
        )
    for zone in range(half):
        side_ref[zone] = project(near_ref[zone], of_core(core, 1, zone))
        own_ref[zone] = project(stay_ref[zone], of_core(core, 0, zone))


def tied(first, second):
    first, second = list(first), list(second)
    both = lax.optimization_barrier(tuple(first + second))
    return list(both[: len(first)]), list(both[len(first) :])


def gather_slots(piece, size, ahead):
    bits = size.bit_length() - 1
    direct = min(bits, 4)
    have = {0: piece}
    for level in range(1, direct):
        if level == 2:
            first = [1 << bit for bit in reversed(range(1, direct))]
            values = lax.optimization_barrier(tuple(have[slot] for slot in first))
            have.update(zip(first, values))
        for slot in range(0, 1 << direct, 2):
            if slot.bit_count() == level:
                along = slot & -slot if slot >> direct - 1 else 1 << slot.bit_length() - 1
                have[slot] = swap(have[slot ^ along], along, size)
    pieces = [(have[slot], [slot]) for slot in sorted(have, key=lambda slot: (slot.bit_count(), slot))]
    for bit in range(4, bits):
        whole = jnp.concatenate([value for value, _ in pieces])
        slots = [slot for _, held in pieces for slot in held]
        pieces = [(whole, slots), (swap(whole, 1 << bit, size), [slot | 1 << bit for slot in slots])]
    return pieces


def per_device(traces, sketch):
    size = lax.axis_size("rcv")
    me = lax.axis_index("rcv")
    rows, sources = traces.shape[1:]
    count, share = sketch.shape[1:]
    zones = size // GROUPS
    half = zones // 2
    bits = size.bit_length() - 1
    chunk = lambda slots: jax.ShapeDtypeStruct((slots, 2 * rows, share), traces.dtype)

    stay, near, far, cross, peak, *core = pl.pallas_call(
        functools.partial(chunk_kernel, share),
        out_shape=(
            chunk(zones),
            chunk(half),
            chunk(half),
            chunk(half),
            jax.ShapeDtypeStruct((1, sources), jnp.float32),
        )
        + (chunk(zones // PARTS),) * (2 * PARTS),
        in_specs=[SMEM, VMEM],
        out_specs=(VMEM,) * (5 + 2 * PARTS),
        scratch_shapes=[pltpu.VMEM((GROUPS, zones, 2 * rows, share), traces.dtype)],
        compiler_params=PARAMS,
        name="source_chunks",
    )(me.astype(jnp.int32).reshape(1), traces)
    core_in = [swap(value, 1, size) for value in core]
    piece = pl.pallas_call(
        fold_kernel,
        out_shape=jax.ShapeDtypeStruct((1, *folded_shape(2 * count, share)), sketch.dtype),
        in_specs=[VMEM],
        out_specs=VMEM,
        compiler_params=PARAMS,
        name="fold_columns",
    )(sketch)
    pieces = gather_slots(piece, size, stay)
    values = [value for value, _ in pieces]
    held = {slot: (which, at) for which, (_, slots) in enumerate(pieces) for at, slot in enumerate(slots)}
    partial = pl.pallas_call(
        functools.partial(sketch_kernel, held),
        out_shape=jax.ShapeDtypeStruct((2, 2, rows, count + 1), jnp.float32),
        in_specs=[VMEM] * (4 + 2 * PARTS + len(values)),
        out_specs=VMEM,
        compiler_params=PARAMS,
        name="sketch_rows",
    )(peak, stay, near, far, *core_in, *values)
    packet = jax.ShapeDtypeStruct((count + 2 * rows, count + 1), jnp.float32)
    own_packet, core_packet = pl.pallas_call(
        gram_kernel,
        out_shape=(packet, packet),
        in_specs=[VMEM] * 2,
        out_specs=(VMEM, VMEM),
        compiler_params=PARAMS,
        name="chip_gram",
    )(partial, swap(partial, 1, size))

    beside = swap(own_packet, 2, size)
    known = [own_packet, core_packet, beside, swap(beside, 1, size)]
    (far_out, cross_out), _ = tied([far, cross], [own_packet])
    far_in, cross_in = swap(far_out, 2, size), swap(cross_out, 3, size)
    gram = own_packet[:count] + beside[:count]
    for bit in range(2, bits):
        gram = gram + swap(gram, 1 << bit, size)

    basis, *weights = pl.pallas_call(
        functools.partial(basis_kernel, math.sqrt(rows * size)),
        out_shape=(jax.ShapeDtypeStruct((2, rows, count), jnp.float32),)
        + (jax.ShapeDtypeStruct((2 * count, 2 * rows), jnp.bfloat16),) * GROUPS,
        in_specs=[VMEM] * (1 + GROUPS),
        out_specs=(VMEM,) * (1 + GROUPS),
        compiler_params=PARAMS,
        cost_estimate=pl.CostEstimate(flops=1_500_000_000, bytes_accessed=1_000_000, transcendentals=0),
        name="orthonormal_basis",
    )(*known, gram)
    folded = folded_shape(2 * count, share)
    bound = 1.01 * math.sqrt(2 * rows * size)
    own, side, *away = pl.pallas_call(
        functools.partial(project_kernel, bound),
        out_shape=(
            jax.ShapeDtypeStruct((half, *folded), jnp.float32),
            jax.ShapeDtypeStruct((half, *folded), jnp.float32),
        )
        + (jax.ShapeDtypeStruct(folded, jnp.float32),) * half,
        in_specs=[VMEM] * (1 + GROUPS + 4 + 2 * PARTS),
        out_specs=(VMEM,) * (2 + half),
        compiler_params=PARAMS,
        name="project_rows",
    )(gram, *weights, stay, near, far_in, cross_in, *core_in)

    send = lambda value, mask: swap(value.astype(jnp.float16), mask, size).astype(jnp.float32)
    if zones <= 4:
        side = send(side, 2)
        parts = [send(away[zone], GROUPS * (half + zone)) for zone in reversed(range(half))]
        parts += [send(own[zone] + side[zone], GROUPS * zone) for zone in range(1, half)]
        total = own[0] + side[0] + sum(parts)
    else:
        total = own + send(side, 2) + send(jnp.stack(away), GROUPS * half)
        while total.shape[0] > 1:
            low, high = jnp.split(total, 2)
            total = low + send(high, GROUPS * low.shape[0])
        total = total[0]
    level = gram[:1, count:] * bound
    total = total * (level / TOP)
    total = unfold(total, 2 * count, share)
    return basis, total.reshape(2, count, share)


def solution(mesh):
    return jax.shard_map(
        per_device,
        mesh=mesh,
        in_specs=(P(None, ("grp", "rcv"), None), P(None, None, "rcv")),
        out_specs=(P(None, ("grp", "rcv"), None), P(None, "grp", "rcv")),
        check_vma=False,
    )
```
